128 devices in a mesh: lat: 8 (over y_hi, z), lon: 16 (over x, y_lo, core).
Axes of the slice: x: 4, y: 4 (y_hi: 2, y_lo: 2; y = y_hi * 2 + y_lo), z: 4, core: 2. Of those that a mesh axis runs over, the one named last changes fastest.
Arguments:
- tokens: bfloat16 [128, 256, 3, 512], P('lat', 'lon'), may hold values from -8 to 8
- w_query: bfloat16 [512, 512], replicated, may hold values from -0.25 to 0.25
- w_key: bfloat16 [512, 512], replicated, may hold values from -0.25 to 0.25
- w_value: bfloat16 [512, 512], replicated, may hold values from -0.25 to 0.25
- w_out: bfloat16 [512, 512], replicated, may hold values from -0.25 to 0.25
- grad_out: bfloat16 [128, 256, 3, 512], P('lat', 'lon'), may hold values from -6 to 6
Outputs:
- grad_tokens: bfloat16 [128, 256, 3, 512], P('lat', 'lon')
- grad_w_query: float32 [512, 512], replicated
- grad_w_key: float32 [512, 512], replicated
- grad_w_value: float32 [512, 512], replicated
- grad_w_out: float32 [512, 512], replicated
The draws below stay inside these ranges and needn't reach their ends.
All inputs are finite; a program needn't handle non-finite values.
Results may differ from the reference program's by a relative error of at most 0.023.
The reference program's roundings to bfloat16 on the way count: a program that leaves them out, or rounds other values in their place, can miss the bound.
Values may be sent and summed in bfloat16 or wider, within the bound.
A program may use at most 128 MiB of HBM per device.

```python
import jax
import jax.numpy as jnp
from jax import lax

D = 512
HEADS = 8
LEV = 3
NLAT = 128
NLON = 256


def draw_tokens(key, part):
    key = jax.random.fold_in(key, 7)
    first_key = jax.random.fold_in(key, 0)
    full_shape = (NLAT, NLON, LEV, D)
    return jnp.clip(jax.random.normal(first_key, full_shape, jnp.float32), -6.0, 6.0).astype(jnp.bfloat16)


def level_of(rng, shape, shards, least, high):
    factor_of = 1.0
    for dim, blocks in shards:
        heights = jax.random.uniform(jax.random.fold_in(jax.random.fold_in(rng, 6), dim), (blocks,), jnp.float32, least / len(shards), high / len(shards))
        factor_of = factor_of * jnp.repeat(jnp.exp(heights), shape[dim] // blocks).reshape((-1,) + (1,) * (len(shape) - 1 - dim))
    return factor_of


def normal_values(own_key, shape, deviation, bound, pieces=(), kind=jnp.bfloat16):
    result = deviation * jax.random.normal(own_key, shape, jnp.float32)
    if pieces:
        result = result * level_of(own_key, shape, pieces, -0.22, 0.18)
    return jnp.clip(result, -bound, bound).astype(kind)


def setup_inputs(seed: int = 0) -> dict:
    splits = jax.random.split(jax.random.key(seed), 7)
    tokens = draw_tokens(jax.random.fold_in(splits[6], 71), 0)
    w_query = normal_values(splits[1], (D, D), D ** -0.5, 0.25)
    w_key = normal_values(splits[2], (D, D), D ** -0.5, 0.25)
    w_value = normal_values(splits[3], (D, D), D ** -0.5, 0.25)
    w_out = normal_values(splits[4], (D, D), D ** -0.5, 0.25)
    grad_out = normal_values(splits[5], (NLAT, NLON, LEV, D), 1.0, 6.0, ((0, 8), (1, 16)))
    return {"tokens": tokens, "w_query": w_query, "w_key": w_key, "w_value": w_value, "w_out": w_out, "grad_out": grad_out}


rim_width = 6
win_span = 13
tile_edge = 8

def tile_mask(row_start, lat_total, levels):
    fill_query = jnp.zeros((tile_edge, tile_edge, levels), jnp.int32)
    query_row = (jnp.arange(tile_edge, dtype=jnp.int32)[:, None, None] + fill_query).reshape(-1)
    query_col = (jnp.arange(tile_edge, dtype=jnp.int32)[None, :, None] + fill_query).reshape(-1)
    tile_span = tile_edge + 2 * rim_width
    fill_key = jnp.zeros((tile_span, tile_span, levels), jnp.int32)
    key_row = (jnp.arange(tile_span, dtype=jnp.int32)[:, None, None] + fill_key).reshape(-1)
    key_col = (jnp.arange(tile_span, dtype=jnp.int32)[None, :, None] + fill_key).reshape(-1)
    query_lat = row_start + query_row
    window_start = jnp.clip(query_lat - rim_width, 0, lat_total - win_span)
    key_lat = row_start - rim_width + key_row
    lat_inside = (key_lat[None, :] >= window_start[:, None]) & (key_lat[None, :] < window_start[:, None] + win_span)
    offset = key_col[None, :] - rim_width - query_col[:, None]
    lon_inside = jnp.abs(offset) <= rim_width
    return lat_inside & lon_inside

def tile_grad(queries, keyvals, upstream, allowed, head_count):
    model_width = queries.shape[1]
    head_dim = model_width // head_count
    score_scale = head_dim ** (-0.5)
    query_count = queries.shape[0]
    q_heads = queries.reshape(query_count, head_count, head_dim).astype(jnp.float32)
    k_heads = keyvals[:, :model_width].reshape(-1, head_count, head_dim).astype(jnp.float32)
    v_heads = keyvals[:, model_width:].reshape(-1, head_count, head_dim).astype(jnp.float32)
    g_heads = upstream.reshape(query_count, head_count, head_dim).astype(jnp.float32)
    scores = jnp.einsum('qhd,khd->hqk', q_heads, k_heads) * score_scale
    scores = jnp.where(allowed[None], scores, -jnp.inf)
    row_max = lax.optimization_barrier(jnp.max(scores, axis=-1, keepdims=True))
    shifted = jnp.exp(scores - row_max)
    attn_prob = shifted / lax.optimization_barrier(jnp.sum(shifted, axis=-1, keepdims=True))
    prob_low = attn_prob.astype(jnp.bfloat16)
    attended = jnp.einsum('hqk,khd->qhd', prob_low.astype(jnp.float32), v_heads).astype(jnp.bfloat16)
    row_dot = lax.optimization_barrier(jnp.sum(g_heads * attended.astype(jnp.float32), axis=-1))
    grad_prob = jnp.einsum('qhd,khd->hqk', g_heads, v_heads)
    grad_score = (attn_prob * (grad_prob - row_dot.T[:, :, None])).astype(jnp.bfloat16).astype(jnp.float32)
    grad_query = jnp.einsum('hqk,khd->qhd', grad_score, k_heads) * score_scale
    grad_key = jnp.einsum('hqk,qhd->khd', grad_score, q_heads) * score_scale
    grad_value = jnp.einsum('hqk,qhd->khd', prob_low.astype(jnp.float32), g_heads)
    key_count = keyvals.shape[0]
    grad_kv = jnp.concatenate([grad_key.reshape(key_count, model_width), grad_value.reshape(key_count, model_width)], axis=1)
    return (attended.reshape(query_count, model_width), grad_query.reshape(query_count, model_width), grad_kv)

def reference(tokens, w_query, w_key, w_value, w_out, grad_out):
    grid_shape = (NLAT, NLON, LEV, D)
    flat_tokens = tokens.reshape(-1, D)
    flat_grad = grad_out.reshape(-1, D)
    query = jnp.dot(flat_tokens, w_query, preferred_element_type=jnp.float32).astype(jnp.bfloat16).reshape(grid_shape)
    key_proj = jnp.dot(flat_tokens, w_key, preferred_element_type=jnp.float32).astype(jnp.bfloat16).reshape(grid_shape)
    value_proj = jnp.dot(flat_tokens, w_value, preferred_element_type=jnp.float32).astype(jnp.bfloat16).reshape(grid_shape)
    upstream = jnp.dot(flat_grad, w_out.T, preferred_element_type=jnp.float32).astype(jnp.bfloat16).reshape(grid_shape)
    keyvals = jnp.concatenate([key_proj, value_proj], axis=-1)
    keyvals = jnp.concatenate([keyvals[:, NLON - rim_width:], keyvals, keyvals[:, :rim_width]], axis=1)
    keyvals = jnp.pad(keyvals, ((rim_width, rim_width), (0, 0), (0, 0), (0, 0)))
    tiles_lon = NLON // tile_edge
    tile_count = NLAT // tile_edge * tiles_lon
    tile_span = tile_edge + 2 * rim_width
    zero_index = jnp.zeros((), jnp.int32)

    def one_tile(index, carry):
        attended_all, grad_query_all, grad_kv_all = carry
        index = jnp.asarray(index).astype(jnp.int32)
        row_first = index // tiles_lon * tile_edge
        col_first = index % tiles_lon * tile_edge
        starts = (row_first, col_first, zero_index, zero_index)
        query_tile = lax.dynamic_slice(query, starts, (tile_edge, tile_edge, LEV, D)).reshape(-1, D)
        upstream_tile = lax.dynamic_slice(upstream, starts, (tile_edge, tile_edge, LEV, D)).reshape(-1, D)
        kv_tile = lax.dynamic_slice(keyvals, starts, (tile_span, tile_span, LEV, 2 * D)).reshape(-1, 2 * D)
        allowed = tile_mask(row_first, NLAT, LEV)
        attended, grad_query, grad_kv = tile_grad(query_tile, kv_tile, upstream_tile, allowed, HEADS)
        attended_all = lax.dynamic_update_slice(attended_all, attended.reshape(tile_edge, tile_edge, LEV, D), starts)
        grad_query_all = lax.dynamic_update_slice(grad_query_all, grad_query.reshape(tile_edge, tile_edge, LEV, D), starts)
        previous = lax.dynamic_slice(grad_kv_all, starts, (tile_span, tile_span, LEV, 2 * D))
        grad_kv_all = lax.dynamic_update_slice(grad_kv_all, previous + grad_kv.reshape(tile_span, tile_span, LEV, 2 * D), starts)
        return (attended_all, grad_query_all, grad_kv_all)
    initial = (jnp.zeros(grid_shape, jnp.bfloat16), jnp.zeros(grid_shape, jnp.float32), jnp.zeros(keyvals.shape, jnp.float32))
    attended_all, grad_query_all, grad_kv_all = lax.fori_loop(0, tile_count, one_tile, initial)
    core = grad_kv_all[rim_width:rim_width + NLAT]
    owned = core[:, rim_width:rim_width + NLON]
    owned = owned.at[:, NLON - rim_width:].add(core[:, :rim_width])
    owned = owned.at[:, :rim_width].add(core[:, NLON + rim_width:])
    grad_query_low = grad_query_all.astype(jnp.bfloat16).reshape(-1, D)
    grad_key_low = owned[..., :D].astype(jnp.bfloat16).reshape(-1, D)
    grad_value_low = owned[..., D:].astype(jnp.bfloat16).reshape(-1, D)
    grad_tokens = jnp.dot(grad_query_low, w_query.T, preferred_element_type=jnp.float32)
    grad_tokens = grad_tokens + jnp.dot(grad_key_low, w_key.T, preferred_element_type=jnp.float32)
    grad_tokens = grad_tokens + jnp.dot(grad_value_low, w_value.T, preferred_element_type=jnp.float32)
    grad_tokens = grad_tokens.astype(jnp.bfloat16).reshape(grid_shape)
    grad_w_query = jnp.dot(flat_tokens.T, grad_query_low, preferred_element_type=jnp.float32)
    grad_w_key = jnp.dot(flat_tokens.T, grad_key_low, preferred_element_type=jnp.float32)
    grad_w_value = jnp.dot(flat_tokens.T, grad_value_low, preferred_element_type=jnp.float32)
    grad_w_out = jnp.dot(attended_all.reshape(-1, D).T, flat_grad, preferred_element_type=jnp.float32)
    return (grad_tokens, grad_w_query, grad_w_key, grad_w_value, grad_w_out)
```

```python
import functools

import jax
import jax.numpy as jnp
from jax import lax
from jax.experimental import pallas as pl
from jax.experimental.pallas import tpu as pltpu
from jax.sharding import PartitionSpec as P

HEADS = 8
HEAD = 64
D = 512
RIM = 6
SPAN = 13
OWN = 28 * 48
SIDE = 28 * 24
ALL = OWN + 2 * SIDE
TQ = 96
KEYS = 768 + 384
CHUNK = 384
F32 = jnp.float32
BF16 = jnp.bfloat16


def nn(a, b):
    return jnp.dot(a, b, preferred_element_type=F32)


def nt(a, b):
    return lax.dot_general(a, b, (((1,), (1,)), ((), ())), preferred_element_type=F32)


def tn(a, b):
    return lax.dot_general(a, b, (((0,), (0,)), ((), ())), preferred_element_type=F32)


def attention_kernel(
    lat_total,
    row0_ref,
    tok_ref,
    grad_ref,
    wq_ref,
    wk_ref,
    wv_ref,
    wo_ref,
    gt_own_ref,
    gt_wide_ref,
    gwq_ref,
    gwk_ref,
    gwv_ref,
    gwo_ref,
    k_ref,
    v_ref,
    kt_ref,
    vt_ref,
    q_ref,
    u_ref,
    gk_ref,
    gv_ref,
    gq_ref,
    att_ref,
    qbd_ref,
    ubd_ref,
    ubdt_ref,
    bias_ref,
    s_ref,
    p_ref,
):
    row0 = row0_ref[0]
    own_rows = pl.ds(RIM * 48, 768)

    def project(i, carry):
        rows = pl.ds(pl.multiple_of(i * 192, 192), 192)
        x = tok_ref[rows, :]
        k_ref[rows, :] = nn(x, wk_ref[...]).astype(BF16)
        v_ref[rows, :] = nn(x, wv_ref[...]).astype(BF16)
        gk_ref[rows, :] = jnp.zeros((192, D), F32)
        gv_ref[rows, :] = jnp.zeros((192, D), F32)
        return carry

    lax.fori_loop(0, ALL // 192, project, 0)
    for i in range(4):
        x = tok_ref[pl.ds(RIM * 48 + 192 * i, 192), :]
        q = nn(x, wq_ref[...]).astype(BF16).astype(F32) * 0.125
        q_ref[pl.ds(12 * i, 12)] = q.reshape(12, 16, D)
        g = grad_ref[pl.ds(192 * i, 192), :]
        u = nt(g, wo_ref[...]).astype(BF16).astype(F32)
        u_ref[pl.ds(12 * i, 12)] = u.reshape(12, 16, D)

    head_row = lax.broadcasted_iota(jnp.int32, (256, 256), 0)
    feature = lax.broadcasted_iota(jnp.int32, (256, 256), 1)

    def diagonal(n):
        owner = (head_row + 256 * n) // TQ
        return owner == (feature + 128 * n) // HEAD

    def latitude_band(r, carry):
        lowest = jnp.where(row0 == 0, RIM, 0)
        highest = jnp.where(row0 + 16 == lat_total, RIM, 12)
        base = jnp.clip(4 * r, lowest, highest)
        for i in range(2):
            part = pl.ds(pl.multiple_of(base * 48 + 384 * i, 48), 384)
            kt_ref[:, pl.ds(384 * i, 384)] = k_ref[part, :].T
            vt_ref[:, pl.ds(384 * i, 384)] = v_ref[part, :].T
        for c in range(2):
            part = pl.ds(pl.multiple_of(OWN + SIDE * c + base * 24, 48), 384)
            kt_ref[:, pl.ds(768 + 384 * c, 384)] = k_ref[part, :].T
            vt_ref[:, pl.ds(768 + 384 * c, 384)] = v_ref[part, :].T

        for c in range(2):
            starts = [
                pl.multiple_of(base * 48, 48),
                pl.multiple_of(base * 48 + 384, 48),
                pl.multiple_of(OWN + SIDE * c + base * 24, 48),
            ]
            columns = [0, 384, 768 + 384 * c]

            lane = lax.broadcasted_iota(jnp.int32, (1, 512), 1) % TQ
            q_lat = row0 + 4 * r + lane // 24
            first = jnp.clip(q_lat - RIM, 0, lat_total - SPAN) - (row0 + base - RIM)
            q_col = lane % 8
            key = lax.broadcasted_iota(jnp.int32, (768, 1), 0)
            d_lat = key // 48 - first
            d_col = key % 16 - 8 * c - q_col + RIM
            inside = (d_lat >= 0) & (d_lat < SPAN) & (d_col >= 0) & (d_col < SPAN)
            bias_ref[0:768, :] = jnp.where(inside, 0.0, -jnp.inf)
            key = lax.broadcasted_iota(jnp.int32, (384, 1), 0)
            d_lat = key // 24 - first
            d_col = key % 8 + (16 * c - 8) - q_col + RIM
            inside = (d_lat >= 0) & (d_lat < SPAN) & (d_col >= 0) & (d_col < SPAN)
            bias_ref[768:1152, :] = jnp.where(inside, 0.0, -jnp.inf)

            groups = pl.ds(12 * r, 12)
            q_tile = q_ref[groups, 8 * c : 8 * c + 8, :].reshape(TQ, D).astype(BF16)
            u_tile = u_ref[groups, 8 * c : 8 * c + 8, :].reshape(TQ, D).astype(BF16)
            q_all = jnp.concatenate([q_tile] * HEADS, axis=0)
            u_all = jnp.concatenate([u_tile] * HEADS, axis=0)
            for n in range(3):
                keep = diagonal(n)
                block = q_all[256 * n : 256 * n + 256, 128 * n : 128 * n + 256]
                qbd_ref[n] = jnp.where(keep, block, jnp.zeros_like(block))
                block = u_all[256 * n : 256 * n + 256, 128 * n : 128 * n + 256]
                block = jnp.where(keep, block, jnp.zeros_like(block))
                ubd_ref[n] = block
                ubdt_ref[n] = block.astype(F32).T

            att_parts = [None] * HEADS
            gq_parts = [None] * HEADS

            def fold(parts, n, block):
                block = jnp.where(diagonal(n), block, 0.0)
                row = 256 * n
                while row < 256 * n + 256:
                    h = row // TQ
                    end = min(TQ * (h + 1), 256 * n + 256)
                    piece = block[row - 256 * n : end - 256 * n]
                    parts.append((row - TQ * h, end - TQ * h, n, piece))
                    row = end

            att_parts = []
            gq_parts = []
            for n in range(3):
                feats = pl.ds(128 * n, 256)
                bias_lane = (0, 256, 128)[n]
                high = jnp.full((8, 256), -jnp.inf, F32)
                for j in range(3):
                    rows = pl.ds(starts[j], CHUNK)
                    s = nt(k_ref[rows, feats], qbd_ref[n])
                    s = s + bias_ref[pl.ds(CHUNK * j, CHUNK), pl.ds(bias_lane, 256)]
                    s_ref[pl.ds(CHUNK * j, CHUNK), :] = s
                    high = jnp.maximum(high, jnp.max(s.reshape(CHUNK // 8, 8, 256), axis=0))
                high = jnp.max(high, axis=0, keepdims=True)
                total = jnp.zeros((8, 256), F32)
                for j in range(3):
                    part = pl.ds(CHUNK * j, CHUNK)
                    e = jnp.exp(s_ref[part, :] - high)
                    s_ref[part, :] = e
                    total = total + jnp.sum(e.reshape(CHUNK // 8, 8, 256), axis=0)
                scale = 1.0 / jnp.sum(total, axis=0, keepdims=True)
                out_t = jnp.zeros((256, 256), F32)
                for j in range(3):
                    part = pl.ds(CHUNK * j, CHUNK)
                    p = s_ref[part, :] * scale
                    s_ref[part, :] = p
                    p_low = p.astype(BF16)
                    p_ref[part, :] = p_low
                    out_t = out_t + nn(vt_ref[feats, pl.ds(columns[j], CHUNK)], p_low)
                out_t = out_t.astype(BF16).astype(F32)
                row_dot = jnp.sum(out_t * ubdt_ref[n], axis=0, keepdims=True)
                fold(att_parts, n, out_t.T)
                gq_t = jnp.zeros((256, 256), F32)
                for j in range(3):
                    part = pl.ds(CHUNK * j, CHUNK)
                    rows = pl.ds(starts[j], CHUNK)
                    grad_p = nt(v_ref[rows, feats], ubd_ref[n])
                    ds = (s_ref[part, :] * (grad_p - row_dot)).astype(BF16)
                    gv_ref[rows, feats] += nn(p_ref[part, :], ubd_ref[n])
                    gk_ref[rows, feats] += nn(ds, qbd_ref[n])
                    gq_t = gq_t + nn(kt_ref[feats, pl.ds(columns[j], CHUNK)], ds)
                fold(gq_parts, n, gq_t.T)

            for parts, ref, factor in ((att_parts, att_ref, 1.0), (gq_parts, gq_ref, 0.125)):
                ref[groups, 8 * c : 8 * c + 8, :] = jnp.zeros((12, 8, D), F32)
                for begin, end, n, piece in parts:
                    view = (
                        pl.ds(12 * r + begin // 8, (end - begin) // 8),
                        slice(8 * c, 8 * c + 8),
                        slice(128 * n, 128 * n + 256),
                    )
                    ref[view] += (piece * factor).reshape((end - begin) // 8, 8, 256)
        return carry

    lax.fori_loop(0, 4, latitude_band, 0)

    gq_low = gq_ref[...].reshape(768, D).astype(BF16)
    att_low = att_ref[...].reshape(768, D).astype(BF16)
    gwq_ref[...] = tn(tok_ref[own_rows, :], gq_low)
    gwo_ref[...] = tn(att_low, grad_ref[...])
    gwk_ref[...] = jnp.zeros((D, D), F32)
    gwv_ref[...] = jnp.zeros((D, D), F32)

    def finish(i, carry):
        rows = pl.ds(pl.multiple_of(i * 192, 192), 192)
        gk_low = gk_ref[rows, :].astype(BF16)
        gv_low = gv_ref[rows, :].astype(BF16)
        k_ref[rows, :] = gk_low
        v_ref[rows, :] = gv_low
        gk_ref[rows, :] = nt(gk_low, wk_ref[...]) + nt(gv_low, wv_ref[...])
        return carry

    lax.fori_loop(0, ALL // 192, finish, 0)
    for i in range(7):
        rows = pl.ds(384 * i, 384)
        x = tok_ref[rows, :]
        gwk_ref[...] += tn(x, k_ref[rows, :])
        gwv_ref[...] += tn(x, v_ref[rows, :])
    gt_own_ref[...] = gk_ref[own_rows, :] + nt(gq_low, wq_ref[...])
    gt_wide_ref[...] = gk_ref[...].astype(BF16)


def attention(row0, tok_wide, grad_out, w_query, w_key, w_value, w_out, lat_total):
    vmem = pl.BlockSpec(memory_space=pltpu.VMEM)
    weight = jax.ShapeDtypeStruct((D, D), F32)
    return pl.pallas_call(
        functools.partial(attention_kernel, lat_total),
        out_shape=(
            jax.ShapeDtypeStruct((768, D), F32),
            jax.ShapeDtypeStruct((ALL, D), BF16),
            weight,
            weight,
            weight,
            weight,
        ),
        in_specs=[pl.BlockSpec(memory_space=pltpu.SMEM)] + [vmem] * 6,
        out_specs=(vmem,) * 6,
        scratch_shapes=[
            pltpu.VMEM((ALL, D), BF16),
            pltpu.VMEM((ALL, D), BF16),
            pltpu.VMEM((D, 1536), BF16),
            pltpu.VMEM((D, 1536), BF16),
            pltpu.VMEM((48, 16, D), F32),
            pltpu.VMEM((48, 16, D), F32),
            pltpu.VMEM((ALL, D), F32),
            pltpu.VMEM((ALL, D), F32),
            pltpu.VMEM((48, 16, D), F32),
            pltpu.VMEM((48, 16, D), F32),
            pltpu.VMEM((3, 256, 256), BF16),
            pltpu.VMEM((3, 256, 256), BF16),
            pltpu.VMEM((3, 256, 256), F32),
            pltpu.VMEM((KEYS, 512), F32),
            pltpu.VMEM((KEYS, 256), F32),
            pltpu.VMEM((KEYS, 256), BF16),
        ],
        compiler_params=pltpu.CompilerParams(vmem_limit_bytes=56 * 1024 * 1024),
    )(row0, tok_wide, grad_out, w_query, w_key, w_value, w_out)


def shift(x, axis, step, closed):
    count = lax.axis_size(axis)
    pairs = [(i, (i + step) % count) for i in range(count) if closed or 0 <= i + step < count]
    return lax.ppermute(x, axis, pairs)


def on_device(tokens, w_query, w_key, w_value, w_out, grad_out):
    lat_dev = tokens.shape[0]
    lat_total = lat_dev * lax.axis_size("lat")
    x = tokens.transpose(0, 2, 1, 3)
    g = grad_out.transpose(0, 2, 1, 3).reshape(768, D)
    row0 = (lax.axis_index("lat") * lat_dev).astype(jnp.int32).reshape(1)

    above = shift(x[lat_dev - RIM :], "lat", 1, False)
    below = shift(x[:RIM], "lat", -1, False)
    strip = jnp.concatenate([above, x, below], axis=0)
    left = shift(strip[:, :, 8:], "lon", 1, True)
    right = shift(strip[:, :, :8], "lon", -1, True)
    wide = jnp.concatenate(
        [strip.reshape(OWN, D), left.reshape(SIDE, D), right.reshape(SIDE, D)], axis=0
    )

    gt_own, gt_wide, gwq, gwk, gwv, gwo = attention(
        row0, wide, g, w_query, w_key, w_value, w_out, lat_total
    )

    gwq, gwk, gwv, gwo = lax.psum((gwq, gwk, gwv, gwo), ("lat", "lon"))

    strip = gt_wide[:OWN].reshape(28, 3, 16, D)
    from_right = shift(gt_wide[OWN : OWN + SIDE].reshape(28, 3, 8, D), "lon", -1, True)
    from_left = shift(gt_wide[OWN + SIDE :].reshape(28, 3, 8, D), "lon", 1, True)
    add = jnp.concatenate([from_left, from_right], axis=2).astype(F32)
    edge_up = (strip[:RIM].astype(F32) + add[:RIM]).astype(BF16)
    edge_down = (strip[RIM + lat_dev :].astype(F32) + add[RIM + lat_dev :]).astype(BF16)
    to_up = shift(edge_up, "lat", -1, False).astype(F32)
    to_down = shift(edge_down, "lat", 1, False).astype(F32)
    total = gt_own.reshape(16, 3, 16, D) + add[RIM : RIM + lat_dev]
    middle = jnp.zeros((lat_dev - 2 * RIM, 3, 16, D), F32)
    total = total + jnp.concatenate([to_down, middle, to_up], axis=0)
    grad_tokens = total.astype(BF16).transpose(0, 2, 1, 3)
    return grad_tokens, gwq, gwk, gwv, gwo


def solution(mesh):
    placed = (P("lat", "lon", None, None), P(), P(), P(), P(), P("lat", "lon", None, None))
    return jax.shard_map(
        on_device,
        mesh=mesh,
        in_specs=placed,
        out_specs=(P("lat", "lon", None, None), P(), P(), P(), P()),
        check_vma=False,
    )
```

```python
import functools

import jax
import jax.numpy as jnp
from jax import lax
from jax.experimental import pallas as pl
from jax.experimental.pallas import tpu as pltpu
from jax.sharding import PartitionSpec as P

HEADS = 8
HEAD = 64
D = 512
RIM = 6
SPAN = 13
OWN = 28 * 48
SIDE = 28 * 24
ALL = OWN + 2 * SIDE
TQ = 96
KEYS = 768 + 384
CHUNK = 384
PARTS = 4
WIDTH = D // PARTS
MESH = pl.DeviceIdType.MESH
F32 = jnp.float32
BF16 = jnp.bfloat16


def nn(a, b):
    return jnp.dot(a, b, preferred_element_type=F32)


def nt(a, b):
    return lax.dot_general(a, b, (((1,), (1,)), ((), ())), preferred_element_type=F32)


def tn(a, b):
    return lax.dot_general(a, b, (((0,), (0,)), ((), ())), preferred_element_type=F32)


def attention_kernel(
    lat_total,
    row0_ref,
    tok_ref,
    grad_ref,
    wq_ref,
    wk_ref,
    wv_ref,
    wo_ref,
    gt_own_ref,
    gt_wide_ref,
    gw_ref,
    k_ref,
    v_ref,
    kt_ref,
    vt_ref,
    q_ref,
    u_ref,
    gk_ref,
    gv_ref,
    gq_ref,
    att_ref,
    qbd_ref,
    ubd_ref,
    ubdt_ref,
    bias_ref,
    s_ref,
    p_ref,
):
    row0 = row0_ref[0]
    own_rows = pl.ds(RIM * 48, 768)

    def project(i, carry):
        rows = pl.ds(pl.multiple_of(i * 192, 192), 192)
        x = tok_ref[rows, :]
        k_ref[rows, :] = nn(x, wk_ref[...]).astype(BF16)
        v_ref[rows, :] = nn(x, wv_ref[...]).astype(BF16)
        gk_ref[rows, :] = jnp.zeros((192, D), F32)
        gv_ref[rows, :] = jnp.zeros((192, D), F32)
        return carry

    lax.fori_loop(0, ALL // 192, project, 0)
    for i in range(4):
        x = tok_ref[pl.ds(RIM * 48 + 192 * i, 192), :]
        q = nn(x, wq_ref[...]).astype(BF16).astype(F32) * 0.125
        q_ref[pl.ds(12 * i, 12)] = q.reshape(12, 16, D)
        g = grad_ref[pl.ds(192 * i, 192), :]
        u = nt(g, wo_ref[...]).astype(BF16).astype(F32)
        u_ref[pl.ds(12 * i, 12)] = u.reshape(12, 16, D)

    head_row = lax.broadcasted_iota(jnp.int32, (256, 256), 0)
    feature = lax.broadcasted_iota(jnp.int32, (256, 256), 1)

    def diagonal(n):
        owner = (head_row + 256 * n) // TQ
        return owner == (feature + 128 * n) // HEAD

    def latitude_band(r, carry):
        lowest = jnp.where(row0 == 0, RIM, 0)
        highest = jnp.where(row0 + 16 == lat_total, RIM, 12)
        base = jnp.clip(4 * r, lowest, highest)
        for i in range(2):
            part = pl.ds(pl.multiple_of(base * 48 + 384 * i, 48), 384)
            kt_ref[:, pl.ds(384 * i, 384)] = k_ref[part, :].T
            vt_ref[:, pl.ds(384 * i, 384)] = v_ref[part, :].T
        for c in range(2):
            part = pl.ds(pl.multiple_of(OWN + SIDE * c + base * 24, 48), 384)
            kt_ref[:, pl.ds(768 + 384 * c, 384)] = k_ref[part, :].T
            vt_ref[:, pl.ds(768 + 384 * c, 384)] = v_ref[part, :].T

        for c in range(2):
            starts = [
                pl.multiple_of(base * 48, 48),
                pl.multiple_of(base * 48 + 384, 48),
                pl.multiple_of(OWN + SIDE * c + base * 24, 48),
            ]
            columns = [0, 384, 768 + 384 * c]

            lane = lax.broadcasted_iota(jnp.int32, (1, 512), 1) % TQ
            q_lat = row0 + 4 * r + lane // 24
            first = jnp.clip(q_lat - RIM, 0, lat_total - SPAN) - (row0 + base - RIM)
            q_col = lane % 8
            key = lax.broadcasted_iota(jnp.int32, (768, 1), 0)
            d_lat = key // 48 - first
            d_col = key % 16 - 8 * c - q_col + RIM
            inside = (d_lat >= 0) & (d_lat < SPAN) & (d_col >= 0) & (d_col < SPAN)
            bias_ref[0:768, :] = jnp.where(inside, 0.0, -jnp.inf)
            key = lax.broadcasted_iota(jnp.int32, (384, 1), 0)
            d_lat = key // 24 - first
            d_col = key % 8 + (16 * c - 8) - q_col + RIM
            inside = (d_lat >= 0) & (d_lat < SPAN) & (d_col >= 0) & (d_col < SPAN)
            bias_ref[768:1152, :] = jnp.where(inside, 0.0, -jnp.inf)

            groups = pl.ds(12 * r, 12)
            q_tile = q_ref[groups, 8 * c : 8 * c + 8, :].reshape(TQ, D).astype(BF16)
            u_tile = u_ref[groups, 8 * c : 8 * c + 8, :].reshape(TQ, D).astype(BF16)
            q_all = jnp.concatenate([q_tile] * HEADS, axis=0)
            u_all = jnp.concatenate([u_tile] * HEADS, axis=0)
            for n in range(3):
                keep = diagonal(n)
                block = q_all[256 * n : 256 * n + 256, 128 * n : 128 * n + 256]
                qbd_ref[n] = jnp.where(keep, block, jnp.zeros_like(block))
                block = u_all[256 * n : 256 * n + 256, 128 * n : 128 * n + 256]
                block = jnp.where(keep, block, jnp.zeros_like(block))
                ubd_ref[n] = block
                ubdt_ref[n] = block.astype(F32).T

            att_parts = [None] * HEADS
            gq_parts = [None] * HEADS

            def fold(parts, n, block):
                block = jnp.where(diagonal(n), block, 0.0)
                row = 256 * n
                while row < 256 * n + 256:
                    h = row // TQ
                    end = min(TQ * (h + 1), 256 * n + 256)
                    piece = block[row - 256 * n : end - 256 * n]
                    parts.append((row - TQ * h, end - TQ * h, n, piece))
                    row = end

            att_parts = []
            gq_parts = []
            for n in range(3):
                feats = pl.ds(128 * n, 256)
                bias_lane = (0, 256, 128)[n]
                high = jnp.full((8, 256), -jnp.inf, F32)
                for j in range(3):
                    rows = pl.ds(starts[j], CHUNK)
                    s = nt(k_ref[rows, feats], qbd_ref[n])
                    s = s + bias_ref[pl.ds(CHUNK * j, CHUNK), pl.ds(bias_lane, 256)]
                    s_ref[pl.ds(CHUNK * j, CHUNK), :] = s
                    high = jnp.maximum(high, jnp.max(s.reshape(CHUNK // 8, 8, 256), axis=0))
                high = jnp.max(high, axis=0, keepdims=True)
                total = jnp.zeros((8, 256), F32)
                for j in range(3):
                    part = pl.ds(CHUNK * j, CHUNK)
                    e = jnp.exp(s_ref[part, :] - high)
                    s_ref[part, :] = e
                    total = total + jnp.sum(e.reshape(CHUNK // 8, 8, 256), axis=0)
                scale = 1.0 / jnp.sum(total, axis=0, keepdims=True)
                out_t = jnp.zeros((256, 256), F32)
                for j in range(3):
                    part = pl.ds(CHUNK * j, CHUNK)
                    p = s_ref[part, :] * scale
                    s_ref[part, :] = p
                    p_low = p.astype(BF16)
                    p_ref[part, :] = p_low
                    out_t = out_t + nn(vt_ref[feats, pl.ds(columns[j], CHUNK)], p_low)
                out_t = out_t.astype(BF16).astype(F32)
                row_dot = jnp.sum(out_t * ubdt_ref[n], axis=0, keepdims=True)
                fold(att_parts, n, out_t.T)
                gq_t = jnp.zeros((256, 256), F32)
                for j in range(3):
                    part = pl.ds(CHUNK * j, CHUNK)
                    rows = pl.ds(starts[j], CHUNK)
                    grad_p = nt(v_ref[rows, feats], ubd_ref[n])
                    ds = (s_ref[part, :] * (grad_p - row_dot)).astype(BF16)
                    gv_ref[rows, feats] += nn(p_ref[part, :], ubd_ref[n])
                    gk_ref[rows, feats] += nn(ds, qbd_ref[n])
                    gq_t = gq_t + nn(kt_ref[feats, pl.ds(columns[j], CHUNK)], ds)
                fold(gq_parts, n, gq_t.T)

            for parts, ref, factor in ((att_parts, att_ref, 1.0), (gq_parts, gq_ref, 0.125)):
                ref[groups, 8 * c : 8 * c + 8, :] = jnp.zeros((12, 8, D), F32)
                for begin, end, n, piece in parts:
                    view = (
                        pl.ds(12 * r + begin // 8, (end - begin) // 8),
                        slice(8 * c, 8 * c + 8),
                        slice(128 * n, 128 * n + 256),
                    )
                    ref[view] += (piece * factor).reshape((end - begin) // 8, 8, 256)
        return carry

    lax.fori_loop(0, 4, latitude_band, 0)

    gq_low = gq_ref[...].reshape(768, D).astype(BF16)
    att_low = att_ref[...].reshape(768, D).astype(BF16)

    def put(index, value):
        for part in range(PARTS):
            columns = value[:, WIDTH * part : WIDTH * part + WIDTH]
            gw_ref[part, pl.ds(D * index, D), :] = columns.astype(BF16)

    put(0, tn(tok_ref[own_rows, :], gq_low))
    put(3, tn(att_low, grad_ref[...]))

    def finish(i, carry):
        rows = pl.ds(pl.multiple_of(i * 192, 192), 192)
        gk_low = gk_ref[rows, :].astype(BF16)
        gv_low = gv_ref[rows, :].astype(BF16)
        k_ref[rows, :] = gk_low
        v_ref[rows, :] = gv_low
        gk_ref[rows, :] = nt(gk_low, wk_ref[...]) + nt(gv_low, wv_ref[...])
        return carry

    lax.fori_loop(0, ALL // 192, finish, 0)
    put(1, tn(tok_ref[...], k_ref[...]))
    put(2, tn(tok_ref[...], v_ref[...]))
    gt_own_ref[...] = gk_ref[own_rows, :] + nt(gq_low, wq_ref[...])
    gt_wide_ref[...] = gk_ref[...].astype(BF16)


def attention(row0, tok_wide, grad_out, w_query, w_key, w_value, w_out, lat_total):
    vmem = pl.BlockSpec(memory_space=pltpu.VMEM)
    return pl.pallas_call(
        functools.partial(attention_kernel, lat_total),
        out_shape=(
            jax.ShapeDtypeStruct((768, D), F32),
            jax.ShapeDtypeStruct((ALL, D), BF16),
            jax.ShapeDtypeStruct((PARTS, 4 * D, WIDTH), BF16),
        ),
        in_specs=[pl.BlockSpec(memory_space=pltpu.SMEM)] + [vmem] * 6,
        out_specs=(vmem,) * 3,
        scratch_shapes=[
            pltpu.VMEM((ALL, D), BF16),
            pltpu.VMEM((ALL, D), BF16),
            pltpu.VMEM((D, 1536), BF16),
            pltpu.VMEM((D, 1536), BF16),
            pltpu.VMEM((48, 16, D), F32),
            pltpu.VMEM((48, 16, D), F32),
            pltpu.VMEM((ALL, D), F32),
            pltpu.VMEM((ALL, D), F32),
            pltpu.VMEM((48, 16, D), F32),
            pltpu.VMEM((48, 16, D), F32),
            pltpu.VMEM((3, 256, 256), BF16),
            pltpu.VMEM((3, 256, 256), BF16),
            pltpu.VMEM((3, 256, 256), F32),
            pltpu.VMEM((KEYS, 512), F32),
            pltpu.VMEM((KEYS, 256), F32),
            pltpu.VMEM((KEYS, 256), BF16),
        ],
        compiler_params=pltpu.CompilerParams(vmem_limit_bytes=56 * 1024 * 1024),
    )(row0, tok_wide, grad_out, w_query, w_key, w_value, w_out)


class Place:
    def __init__(self):
        self.lat = lax.axis_index("lat")
        self.lon = lax.axis_index("lon")
        self.z = self.lat % 4
        self.core = self.lon % 2
        self.x = self.lon // 4
        self.y = (self.lat // 4) * 2 + (self.lon // 2) % 2
        self.inside = {-1: self.lat > 0, 0: None, 1: self.lat < 7}

    def near(self, dlat, dlon):
        return (self.lat + dlat, lax.rem(self.lon + dlon + 16, 16))

    def along(self, axis, step):
        x, y, z = self.x, self.y, self.z
        if axis == "x":
            x = lax.rem(x + step, 4)
        elif axis == "y":
            y = lax.rem(y + step, 4)
        else:
            z = lax.rem(z + step, 4)
        return ((y // 2) * 4 + z, x * 4 + (y % 2) * 2 + self.core)

    def other_core(self):
        return (self.lat, self.lon + 1 - 2 * self.core)

    def index(self, axis):
        return {"x": self.x, "y": self.y, "z": self.z}[axis]


def guarded(condition, action):
    if condition is None:
        action()
    else:
        pl.when(condition)(action)


def halo_copies(place, send_sem, recv_sem, routes):
    copies = []
    for i, (dlat, dlon, source, target) in enumerate(routes):
        copy = pltpu.make_async_remote_copy(
            src_ref=source,
            dst_ref=target,
            send_sem=send_sem.at[i],
            recv_sem=recv_sem.at[i],
            device_id=place.near(dlat, dlon),
            device_id_type=MESH,
        )
        copies.append((place.inside[dlat], place.inside[-dlat], copy))
    return copies


def greet(place):
    barrier = pltpu.get_barrier_semaphore()
    for dlat in (-1, 0, 1):
        for dlon in (-1, 0, 1):
            if dlat or dlon:

                def signal(dlat=dlat, dlon=dlon):
                    pl.semaphore_signal(
                        barrier, inc=1, device_id=place.near(dlat, dlon), device_id_type=MESH
                    )

                guarded(place.inside[dlat], signal)
    rows = jnp.where(place.lat > 0, 3, 0) + jnp.where(place.lat < 7, 3, 0)
    return barrier, 2 + rows


def gather_kernel(x_ref, wide_ref, half_ref, send_sem, recv_sem):
    place = Place()
    barrier, count = greet(place)
    x = x_ref[...].astype(F32).reshape(48, 16, D)
    half_ref[0:384, :] = x[:, 0:8].reshape(384, D).astype(BF16)
    half_ref[384:768, :] = x[:, 8:16].reshape(384, D).astype(BF16)
    pl.semaphore_wait(barrier, count)

    strip_first = {-1: 22, 0: 6, 1: 0}
    rows = {-1: (0, 6), 0: (0, 16), 1: (10, 6)}
    routes = []
    for dlat in (-1, 0, 1):
        begin, count = rows[dlat]
        for dlon in (-1, 0, 1):
            first = strip_first[dlat]
            if dlon == 0:
                if dlat == 0:
                    continue
                source = x_ref.at[pl.ds(48 * begin, 48 * count)]
                target = wide_ref.at[pl.ds(48 * first, 48 * count)]
            else:
                half = 384 if dlon == 1 else 0
                side = OWN if dlon == 1 else OWN + SIDE
                source = half_ref.at[pl.ds(half + 24 * begin, 24 * count)]
                target = wide_ref.at[pl.ds(side + 24 * first, 24 * count)]
            routes.append((dlat, dlon, source, target))
    copies = halo_copies(place, send_sem, recv_sem, routes)
    for sends, _, copy in copies:
        guarded(sends, copy.start)
    wide_ref[pl.ds(RIM * 48, 768), :] = x_ref[...]

    def clear(first):
        wide_ref[pl.ds(48 * first, 288), :] = jnp.zeros((288, D), BF16)
        wide_ref[pl.ds(OWN + 24 * first, 144), :] = jnp.zeros((144, D), BF16)
        wide_ref[pl.ds(OWN + SIDE + 24 * first, 144), :] = jnp.zeros((144, D), BF16)

    pl.when(place.lat == 0)(lambda: clear(0))
    pl.when(place.lat == 7)(lambda: clear(22))
    for sends, receives, copy in copies:
        guarded(sends, copy.wait_send)
        guarded(receives, copy.wait_recv)


def gather(x):
    vmem = pl.BlockSpec(memory_space=pltpu.VMEM)
    return pl.pallas_call(
        gather_kernel,
        out_shape=jax.ShapeDtypeStruct((ALL, D), BF16),
        in_specs=[vmem],
        out_specs=vmem,
        scratch_shapes=[
            pltpu.VMEM((768, D), BF16),
            pltpu.SemaphoreType.DMA((8,)),
            pltpu.SemaphoreType.DMA((8,)),
        ],
        compiler_params=pltpu.CompilerParams(
            collective_id=0, has_side_effects=True, vmem_limit_bytes=24 * 1024 * 1024
        ),
    )(x)


ORDERS = (("x", "y", "z"), ("y", "z", "x"), ("z", "x", "y"), ("x", "z", "y"))
BLOCKS = (256, 64, 16)


def reduce_kernel(
    own_ref,
    wide_ref,
    gw_ref,
    out_ref,
    sum_ref,
    middle_ref,
    sides_ref,
    acc_ref,
    pair_ref,
    send0,
    recv0,
    send1,
    recv1,
    send2,
    recv2,
    halo_send,
    halo_recv,
    pair_send,
    pair_recv,
    ring_send,
    ring_recv,
    back_send,
    back_recv,
    last_send,
    last_recv,
):
    place = Place()
    barrier, count = greet(place)
    partners = [place.other_core()]
    partners += [place.along(axis, step) for axis in "xyz" for step in (1, 2, 3)]
    for partner in partners:
        pl.semaphore_signal(barrier, inc=1, device_id=partner, device_id_type=MESH)
    pl.semaphore_wait(barrier, count + len(partners))

    mine = pl.multiple_of(place.core * 1024, 1024)
    theirs = pl.multiple_of(1024 - place.core * 1024, 1024)
    waits = []

    def send(source, target, send_sem, recv_sem, device):
        copy = pltpu.make_async_remote_copy(
            src_ref=source,
            dst_ref=target,
            send_sem=send_sem,
            recv_sem=recv_sem,
            device_id=device,
            device_id_type=MESH,
        )
        copy.start()
        waits.append(copy)
        return copy

    pair = [
        send(
            gw_ref.at[p, pl.ds(theirs, 1024)],
            pair_ref.at[p],
            pair_send.at[p],
            pair_recv.at[p],
            place.other_core(),
        )
        for p in range(PARTS)
    ]

    strip_first = {-1: 0, 0: 6, 1: 22}
    middle_slot = {-1: 0, 1: 288}
    side_slot = {-1: 0, 0: 144, 1: 528}
    routes = []
    for dlat in (-1, 0, 1):
        rows = 16 if dlat == 0 else 6
        for dlon in (-1, 0, 1):
            first = strip_first[dlat]
            if dlon == 0:
                if dlat == 0:
                    continue
                source = wide_ref.at[pl.ds(48 * first, 48 * rows)]
                target = middle_ref.at[pl.ds(middle_slot[dlat], 48 * rows)]
            else:
                side = OWN if dlon == -1 else OWN + SIDE
                slot = SIDE if dlon == -1 else 0
                source = wide_ref.at[pl.ds(side + 24 * first, 24 * rows)]
                target = sides_ref.at[pl.ds(slot + side_slot[dlat], 24 * rows)]
            routes.append((dlat, dlon, source, target))
    halo = halo_copies(place, halo_send, halo_recv, routes)
    for sends, _, copy in halo:
        guarded(sends, copy.start)

    buffers = ((send0, recv0), (send1, recv1), (send2, recv2))
    pending = [[pair[p]] for p in range(PARTS)]
    base = [0] * PARTS
    for stage in range(3):
        rows = BLOCKS[stage]
        outgoing, incoming = buffers[stage]
        for p in range(PARTS):
            for copy in pending[p]:
                copy.wait_recv()
            if stage == 0:
                acc_ref[p] = gw_ref[p, pl.ds(mine, 1024), :].astype(F32) + pair_ref[p].astype(F32)
            else:
                before = buffers[stage - 1][1]
                here = pl.ds(base[p], BLOCKS[stage - 1])
                total = acc_ref[p, here, :]
                for step in range(3):
                    total = total + before[p, step].astype(F32)
                acc_ref[p, here, :] = total
            axis = ORDERS[p][stage]
            me = place.index(axis)
            pending[p] = []
            for step in (1, 2, 3):
                block = base[p] + lax.rem(me + step, 4) * rows
                block = pl.multiple_of(block, rows)
                outgoing[p, step - 1] = acc_ref[p, pl.ds(block, rows), :].astype(BF16)
                slot = (p * 3 + stage) * 3 + step - 1
                pending[p].append(
                    send(
                        outgoing.at[p, step - 1],
                        incoming.at[p, step - 1],
                        ring_send.at[slot],
                        ring_recv.at[slot],
                        place.along(axis, step),
                    )
                )
            base[p] = pl.multiple_of(base[p] + me * rows, rows)

    for stage in (3, 2, 1, 0):
        for p in range(PARTS):
            for copy in pending[p]:
                copy.wait_recv()
            if stage == 3:
                here = pl.ds(base[p], 16)
                total = acc_ref[p, here, :]
                for step in range(3):
                    total = total + recv2[p, step].astype(F32)
                sum_ref[p, pl.ds(pl.multiple_of(mine + base[p], 16), 16), :] = total.astype(BF16)
            if stage > 0:
                rows = BLOCKS[stage - 1]
                axis = ORDERS[p][stage - 1]
                here = sum_ref.at[p, pl.ds(pl.multiple_of(mine + base[p], rows), rows)]
                pending[p] = []
                for step in (1, 2, 3):
                    slot = (p * 3 + stage - 1) * 3 + step - 1
                    pending[p].append(
                        send(
                            here,
                            here,
                            back_send.at[slot],
                            back_recv.at[slot],
                            place.along(axis, step),
                        )
                    )
                base[p] = base[p] - place.index(axis) * rows
            else:
                here = sum_ref.at[p, pl.ds(mine, 1024)]
                pending[p] = [
                    send(here, here, last_send.at[p], last_recv.at[p], place.other_core())
                ]

    for sends, receives, copy in halo:
        guarded(sends, copy.wait_send)
        guarded(receives, copy.wait_recv)
    for half in range(2):
        part = sides_ref[pl.ds(SIDE * half + 144, 384), :].astype(F32).reshape(48, 8, D)
        own_ref_part = own_ref[:, 8 * half : 8 * half + 8, :]
        acc = own_ref_part + part
        out_ref[:, 8 * half : 8 * half + 8, :] = acc

    def edge(slot, side, first):
        rows = pl.ds(3 * first, 18)
        out_ref[rows] = out_ref[rows] + middle_ref[pl.ds(slot, 288), :].astype(F32).reshape(18, 16, D)
        for half in range(2):
            part = sides_ref[pl.ds(SIDE * half + side, 144), :].astype(F32).reshape(18, 8, D)
            view = out_ref[rows, 8 * half : 8 * half + 8, :]
            out_ref[rows, 8 * half : 8 * half + 8, :] = view + part

    pl.when(place.lat < 7)(lambda: edge(0, 0, 10))
    pl.when(place.lat > 0)(lambda: edge(288, 528, 0))

    for p in range(PARTS):
        pending[p][0].wait_recv()
    for copy in waits:
        copy.wait_send()


def reduce(gt_own, gt_wide, gw):
    vmem = pl.BlockSpec(memory_space=pltpu.VMEM)
    dma = pltpu.SemaphoreType.DMA
    scratch = [
        pltpu.VMEM((576, D), BF16),
        pltpu.VMEM((2 * SIDE, D), BF16),
        pltpu.VMEM((PARTS, 1024, WIDTH), F32),
        pltpu.VMEM((PARTS, 1024, WIDTH), BF16),
    ]
    for rows in BLOCKS:
        scratch += [pltpu.VMEM((PARTS, 3, rows, WIDTH), BF16)] * 2
    for count in (8, PARTS, 9 * PARTS, 9 * PARTS, PARTS):
        scratch += [dma((count,))] * 2
    return pl.pallas_call(
        reduce_kernel,
        out_shape=(
            jax.ShapeDtypeStruct((48, 16, D), F32),
            jax.ShapeDtypeStruct((PARTS, 4 * D, WIDTH), BF16),
        ),
        in_specs=[vmem] * 3,
        out_specs=(vmem,) * 2,
        scratch_shapes=scratch,
        compiler_params=pltpu.CompilerParams(
            collective_id=1, has_side_effects=True, vmem_limit_bytes=40 * 1024 * 1024
        ),
    )(gt_own.reshape(48, 16, D), gt_wide, gw)


def on_device(tokens, w_query, w_key, w_value, w_out, grad_out):
    lat_dev = tokens.shape[0]
    lat_total = lat_dev * lax.axis_size("lat")
    x = tokens.transpose(0, 2, 1, 3).reshape(768, D)
    g = grad_out.transpose(0, 2, 1, 3).reshape(768, D)
    row0 = (lax.axis_index("lat") * lat_dev).astype(jnp.int32).reshape(1)
    wide = gather(x)
    gt_own, gt_wide, gw = attention(row0, wide, g, w_query, w_key, w_value, w_out, lat_total)
    grad_tokens, sums = reduce(gt_own, gt_wide, gw)
    grad_tokens = grad_tokens.reshape(16, 3, 16, D).transpose(0, 2, 1, 3).astype(BF16)
    sums = sums.reshape(PARTS, 4, D, WIDTH).transpose(1, 2, 0, 3).reshape(4, D, D).astype(F32)
    return grad_tokens, sums[0], sums[1], sums[2], sums[3]


def solution(mesh):
    placed = (P("lat", "lon", None, None), P(), P(), P(), P(), P("lat", "lon", None, None))
    return jax.shard_map(
        on_device,
        mesh=mesh,
        in_specs=placed,
        out_specs=(P("lat", "lon", None, None), P(), P(), P(), P()),
        check_vma=False,
    )
```

```python
import functools

import jax
import jax.numpy as jnp
from jax import lax
from jax.experimental import pallas as pl
from jax.experimental.pallas import tpu as pltpu
from jax.sharding import PartitionSpec as P

HEADS = 8
HEAD = 64
D = 512
RIM = 6
SPAN = 13
OWN = 28 * 48
SIDE = 28 * 24
ALL = OWN + 2 * SIDE
TQ = 96
KEYS = 768 + 384
CHUNK = 384
PARTS = 4
WIDTH = D // PARTS
MESH = pl.DeviceIdType.MESH
F32 = jnp.float32
BF16 = jnp.bfloat16


def nn(a, b):
    return jnp.dot(a, b, preferred_element_type=F32)


def nt(a, b):
    return lax.dot_general(a, b, (((1,), (1,)), ((), ())), preferred_element_type=F32)


def tn(a, b):
    return lax.dot_general(a, b, (((0,), (0,)), ((), ())), preferred_element_type=F32)


def attention_kernel(
    lat_total,
    row0_ref,
    tok_ref,
    grad_ref,
    wq_ref,
    wk_ref,
    wv_ref,
    wo_ref,
    gt_own_ref,
    gt_wide_ref,
    gw_ref,
    k_ref,
    v_ref,
    kt_ref,
    vt_ref,
    q_ref,
    u_ref,
    gk_ref,
    gv_ref,
    gq_ref,
    att_ref,
    qbd_ref,
    ubd_ref,
    ubdt_ref,
    bias_ref,
    s_ref,
    p_ref,
    ds_ref,
):
    row0 = row0_ref[0]
    own_rows = pl.ds(RIM * 48, 768)

    def project(i, carry):
        rows = pl.ds(pl.multiple_of(i * 672, 672), 672)
        x = tok_ref[rows, :]
        k_ref[rows, :] = nn(x, wk_ref[...]).astype(BF16)
        v_ref[rows, :] = nn(x, wv_ref[...]).astype(BF16)
        gk_ref[rows, :] = jnp.zeros((672, D), F32)
        gv_ref[rows, :] = jnp.zeros((672, D), F32)
        return carry

    lax.fori_loop(0, ALL // 672, project, 0)
    for i in range(4):
        x = tok_ref[pl.ds(RIM * 48 + 192 * i, 192), :]
        q = nn(x, wq_ref[...]).astype(BF16).astype(F32) * 0.125
        q_ref[pl.ds(12 * i, 12)] = q.reshape(12, 16, D)
        g = grad_ref[pl.ds(192 * i, 192), :]
        u = nt(g, wo_ref[...]).astype(BF16).astype(F32)
        u_ref[pl.ds(12 * i, 12)] = u.reshape(12, 16, D)

    head_row = lax.broadcasted_iota(jnp.int32, (256, 256), 0)
    feature = lax.broadcasted_iota(jnp.int32, (256, 256), 1)

    def diagonal(n):
        owner = (head_row + 256 * n) // TQ
        return owner == (feature + 128 * n) // HEAD

    def latitude_band(r, carry):
        lowest = jnp.where(row0 == 0, RIM, 0)
        highest = jnp.where(row0 + 16 == lat_total, RIM, 12)
        base = jnp.clip(4 * r, lowest, highest)
        own = [pl.multiple_of(base * 48 + 384 * i, 48) for i in range(2)]
        side = [pl.multiple_of(OWN + SIDE * c + base * 24, 48) for c in range(2)]
        for i, start in enumerate((side[0], own[0], own[1], side[1])):
            part = pl.ds(start, CHUNK)
            kt_ref[:, pl.ds(CHUNK * i, CHUNK)] = k_ref[part, :].T
            vt_ref[:, pl.ds(CHUNK * i, CHUNK)] = v_ref[part, :].T
        starts = ((side[0], own[0], own[1]), (own[0], own[1], side[1]))
        groups = pl.ds(12 * r, 12)

        for c in range(2):
            lane = lax.broadcasted_iota(jnp.int32, (1, 512), 1) % TQ
            q_lat = row0 + 4 * r + lane // 24
            first = jnp.clip(q_lat - RIM, 0, lat_total - SPAN) - (row0 + base - RIM)
            q_col = lane % 8

            def bias(d_lat, d_col):
                inside = (d_lat >= 0) & (d_lat < SPAN) & (d_col >= 0) & (d_col < SPAN)
                return jnp.where(inside, 0.0, -jnp.inf)

            key = lax.broadcasted_iota(jnp.int32, (768, 1), 0)
            rows = pl.ds(CHUNK * (1 - c), 768)
            bias_ref[c, rows, :] = bias(key // 48 - first, key % 16 - 8 * c - q_col + RIM)
            key = lax.broadcasted_iota(jnp.int32, (384, 1), 0)
            rows = pl.ds(768 * c, 384)
            bias_ref[c, rows, :] = bias(key // 24 - first, key % 8 + (16 * c - 8) - q_col + RIM)

            q_tile = q_ref[groups, 8 * c : 8 * c + 8, :].reshape(TQ, D).astype(BF16)
            u_tile = u_ref[groups, 8 * c : 8 * c + 8, :].reshape(TQ, D).astype(BF16)
            q_all = jnp.concatenate([q_tile] * HEADS, axis=0)
            u_all = jnp.concatenate([u_tile] * HEADS, axis=0)
            for n in range(3):
                keep = diagonal(n)
                block = q_all[256 * n : 256 * n + 256, 128 * n : 128 * n + 256]
                qbd_ref[3 * c + n] = jnp.where(keep, block, jnp.zeros_like(block))
                block = u_all[256 * n : 256 * n + 256, 128 * n : 128 * n + 256]
                block = jnp.where(keep, block, jnp.zeros_like(block))
                ubd_ref[3 * c + n] = block
                ubdt_ref[3 * c + n] = block.astype(F32).T
            att_ref[groups, 8 * c : 8 * c + 8, :] = jnp.zeros((12, 8, D), F32)
            gq_ref[groups, 8 * c : 8 * c + 8, :] = jnp.zeros((12, 8, D), F32)

        def fold(ref, c, n, block):
            block = jnp.where(diagonal(n), block, 0.0)
            row = 256 * n
            while row < 256 * n + 256:
                h = row // TQ
                end = min(TQ * (h + 1), 256 * n + 256)
                begin = row - TQ * h
                count = (end - row) // 8
                view = (
                    pl.ds(12 * r + begin // 8, count),
                    slice(8 * c, 8 * c + 8),
                    slice(128 * n, 128 * n + 256),
                )
                ref[view] += block[row - 256 * n : end - 256 * n].reshape(count, 8, 256)
                row = end

        state = [{} for _ in range(6)]

        def parts(b):
            return b // 3, b % 3, pl.ds(128 * (b % 3), 256)

        def score(b):
            c, n, feats = parts(b)
            bias_lane = pl.ds((0, 256, 128)[n], 256)
            high = jnp.full((8, 256), -jnp.inf, F32)
            for j in range(3):
                part = pl.ds(CHUNK * j, CHUNK)
                x = nt(k_ref[pl.ds(starts[c][j], CHUNK), feats], qbd_ref[b])
                x = x + bias_ref[c, part, bias_lane]
                s_ref[b, part, :] = x
                high = jnp.maximum(high, jnp.max(x.reshape(CHUNK // 8, 8, 256), axis=0))
                yield
            state[b]["high"] = jnp.max(high, axis=0, keepdims=True)

        def exponent(b):
            high = state[b]["high"]
            total = jnp.zeros((8, 256), F32)
            for j in range(3):
                part = pl.ds(CHUNK * j, CHUNK)
                e = jnp.exp(s_ref[b, part, :] - high)
                s_ref[b, part, :] = e
                total = total + jnp.sum(e.reshape(CHUNK // 8, 8, 256), axis=0)
                yield
            state[b]["scale"] = 1.0 / jnp.sum(total, axis=0, keepdims=True)

        def attend(b):
            c, n, feats = parts(b)
            scale = state[b]["scale"]
            for j in range(3):
                part = pl.ds(CHUNK * j, CHUNK)
                p = s_ref[b, part, :] * scale
                s_ref[b, part, :] = p
                p_ref[b, part, :] = p.astype(BF16)
                yield
            out_t = nn(vt_ref[feats, pl.ds(CHUNK * c, KEYS)], p_ref[b])
            out_t = out_t.astype(BF16).astype(F32)
            state[b]["row_dot"] = jnp.sum(out_t * ubdt_ref[b], axis=0, keepdims=True)
            fold(att_ref, c, n, out_t.T)

        def gradient(b):
            c, n, feats = parts(b)
            row_dot = state[b]["row_dot"]
            for j in range(3):
                part = pl.ds(CHUNK * j, CHUNK)
                rows = pl.ds(starts[c][j], CHUNK)
                grad_p = nt(v_ref[rows, feats], ubd_ref[b])
                ds = (s_ref[b, part, :] * (grad_p - row_dot)).astype(BF16)
                ds_ref[b, part, :] = ds
                gv_ref[rows, feats] += nn(p_ref[b, part, :], ubd_ref[b])
                gk_ref[rows, feats] += nn(ds, qbd_ref[b])
                yield
            gq_t = nn(kt_ref[feats, pl.ds(CHUNK * c, KEYS)], ds_ref[b])
            fold(gq_ref, c, n, gq_t.T)

        stages = (score, exponent, attend, gradient)
        for step in range(6 + len(stages) - 1):
            running = [
                stage(step - i) for i, stage in enumerate(stages) if 0 <= step - i < 6
            ]
            while running:
                running = [g for g in running if next(g, running) is None]
        return carry

    lax.fori_loop(0, 4, latitude_band, 0)

    gq_low = (gq_ref[...].reshape(768, D) * 0.125).astype(BF16)
    att_low = att_ref[...].reshape(768, D).astype(BF16)

    def put(index, value):
        for part in range(PARTS):
            columns = value[:, WIDTH * part : WIDTH * part + WIDTH]
            gw_ref[part, pl.ds(D * index, D), :] = columns.astype(BF16)

    put(0, tn(tok_ref[own_rows, :], gq_low))
    put(3, tn(att_low, grad_ref[...]))

    def finish(i, carry):
        rows = pl.ds(pl.multiple_of(i * 672, 672), 672)
        gk_low = gk_ref[rows, :].astype(BF16)
        gv_low = gv_ref[rows, :].astype(BF16)
        k_ref[rows, :] = gk_low
        v_ref[rows, :] = gv_low
        gk_ref[rows, :] = nt(gk_low, wk_ref[...]) + nt(gv_low, wv_ref[...])
        return carry

    lax.fori_loop(0, ALL // 672, finish, 0)
    put(1, tn(tok_ref[...], k_ref[...]))
    put(2, tn(tok_ref[...], v_ref[...]))
    gt_own_ref[...] = gk_ref[own_rows, :] + nt(gq_low, wq_ref[...])
    gt_wide_ref[...] = gk_ref[...].astype(BF16)


def attention(row0, tok_wide, grad_out, w_query, w_key, w_value, w_out, lat_total):
    vmem = pl.BlockSpec(memory_space=pltpu.VMEM)
    return pl.pallas_call(
        functools.partial(attention_kernel, lat_total),
        out_shape=(
            jax.ShapeDtypeStruct((768, D), F32),
            jax.ShapeDtypeStruct((ALL, D), BF16),
            jax.ShapeDtypeStruct((PARTS, 4 * D, WIDTH), BF16),
        ),
        in_specs=[pl.BlockSpec(memory_space=pltpu.SMEM)] + [vmem] * 6,
        out_specs=(vmem,) * 3,
        scratch_shapes=[
            pltpu.VMEM((ALL, D), BF16),
            pltpu.VMEM((ALL, D), BF16),
            pltpu.VMEM((D, 1536), BF16),
            pltpu.VMEM((D, 1536), BF16),
            pltpu.VMEM((48, 16, D), F32),
            pltpu.VMEM((48, 16, D), F32),
            pltpu.VMEM((ALL, D), F32),
            pltpu.VMEM((ALL, D), F32),
            pltpu.VMEM((48, 16, D), F32),
            pltpu.VMEM((48, 16, D), F32),
            pltpu.VMEM((6, 256, 256), BF16),
            pltpu.VMEM((6, 256, 256), BF16),
            pltpu.VMEM((6, 256, 256), F32),
            pltpu.VMEM((2, KEYS, 512), F32),
            pltpu.VMEM((6, KEYS, 256), F32),
            pltpu.VMEM((6, KEYS, 256), BF16),
            pltpu.VMEM((6, KEYS, 256), BF16),
        ],
        compiler_params=pltpu.CompilerParams(vmem_limit_bytes=60 * 1024 * 1024),
    )(row0, tok_wide, grad_out, w_query, w_key, w_value, w_out)


class Place:
    def __init__(self):
        self.lat = lax.axis_index("lat")
        self.lon = lax.axis_index("lon")
        self.z = self.lat % 4
        self.core = self.lon % 2
        self.x = self.lon // 4
        self.y = (self.lat // 4) * 2 + (self.lon // 2) % 2
        self.inside = {-1: self.lat > 0, 0: None, 1: self.lat < 7}

    def near(self, dlat, dlon):
        return (self.lat + dlat, lax.rem(self.lon + dlon + 16, 16))

    def along(self, axis, step):
        x, y, z = self.x, self.y, self.z
        if axis == "x":
            x = lax.rem(x + step, 4)
        elif axis == "y":
            y = lax.rem(y + step, 4)
        else:
            z = lax.rem(z + step, 4)
        return ((y // 2) * 4 + z, x * 4 + (y % 2) * 2 + self.core)

    def other_core(self):
        return (self.lat, self.lon + 1 - 2 * self.core)

    def index(self, axis):
        return {"x": self.x, "y": self.y, "z": self.z}[axis]


def guarded(condition, action):
    if condition is None:
        action()
    else:
        pl.when(condition)(action)


def halo_copies(place, send_sem, recv_sem, routes):
    copies = []
    for i, (dlat, dlon, source, target) in enumerate(routes):
        copy = pltpu.make_async_remote_copy(
            src_ref=source,
            dst_ref=target,
            send_sem=send_sem.at[i],
            recv_sem=recv_sem.at[i],
            device_id=place.near(dlat, dlon),
            device_id_type=MESH,
        )
        copies.append((place.inside[dlat], place.inside[-dlat], copy))
    return copies


def greet(place):
    barrier = pltpu.get_barrier_semaphore()
    for dlat in (-1, 0, 1):
        for dlon in (-1, 0, 1):
            if dlat or dlon:

                def signal(dlat=dlat, dlon=dlon):
                    pl.semaphore_signal(
                        barrier, inc=1, device_id=place.near(dlat, dlon), device_id_type=MESH
                    )

                guarded(place.inside[dlat], signal)
    rows = jnp.where(place.lat > 0, 3, 0) + jnp.where(place.lat < 7, 3, 0)
    return barrier, 2 + rows


def gather_kernel(x_ref, wide_ref, half_ref, send_sem, recv_sem):
    place = Place()
    barrier, count = greet(place)
    x = x_ref[...].astype(F32).reshape(48, 16, D)
    half_ref[0:384, :] = x[:, 0:8].reshape(384, D).astype(BF16)
    half_ref[384:768, :] = x[:, 8:16].reshape(384, D).astype(BF16)
    pl.semaphore_wait(barrier, count)

    strip_first = {-1: 22, 0: 6, 1: 0}
    rows = {-1: (0, 6), 0: (0, 16), 1: (10, 6)}
    routes = []
    for dlat in (-1, 0, 1):
        begin, count = rows[dlat]
        for dlon in (-1, 0, 1):
            first = strip_first[dlat]
            if dlon == 0:
                if dlat == 0:
                    continue
                source = x_ref.at[pl.ds(48 * begin, 48 * count)]
                target = wide_ref.at[pl.ds(48 * first, 48 * count)]
            else:
                half = 384 if dlon == 1 else 0
                side = OWN if dlon == 1 else OWN + SIDE
                source = half_ref.at[pl.ds(half + 24 * begin, 24 * count)]
                target = wide_ref.at[pl.ds(side + 24 * first, 24 * count)]
            routes.append((dlat, dlon, source, target))
    copies = halo_copies(place, send_sem, recv_sem, routes)
    for sends, _, copy in copies:
        guarded(sends, copy.start)
    wide_ref[pl.ds(RIM * 48, 768), :] = x_ref[...]

    def clear(first):
        wide_ref[pl.ds(48 * first, 288), :] = jnp.zeros((288, D), BF16)
        wide_ref[pl.ds(OWN + 24 * first, 144), :] = jnp.zeros((144, D), BF16)
        wide_ref[pl.ds(OWN + SIDE + 24 * first, 144), :] = jnp.zeros((144, D), BF16)

    pl.when(place.lat == 0)(lambda: clear(0))
    pl.when(place.lat == 7)(lambda: clear(22))
    for sends, receives, copy in copies:
        guarded(sends, copy.wait_send)
        guarded(receives, copy.wait_recv)


def gather(x):
    vmem = pl.BlockSpec(memory_space=pltpu.VMEM)
    return pl.pallas_call(
        gather_kernel,
        out_shape=jax.ShapeDtypeStruct((ALL, D), BF16),
        in_specs=[vmem],
        out_specs=vmem,
        scratch_shapes=[
            pltpu.VMEM((768, D), BF16),
            pltpu.SemaphoreType.DMA((8,)),
            pltpu.SemaphoreType.DMA((8,)),
        ],
        compiler_params=pltpu.CompilerParams(
            collective_id=0, has_side_effects=True, vmem_limit_bytes=24 * 1024 * 1024
        ),
    )(x)


ORDERS = (("x", "y", "z"), ("y", "z", "x"), ("z", "x", "y"), ("x", "z", "y"))
BLOCKS = (256, 64, 16)


def reduce_kernel(
    own_ref,
    wide_ref,
    gw_ref,
    out_ref,
    sum_ref,
    middle_ref,
    sides_ref,
    acc_ref,
    pair_ref,
    send0,
    recv0,
    send1,
    recv1,
    send2,
    recv2,
    halo_send,
    halo_recv,
    pair_send,
    pair_recv,
    ring_send,
    ring_recv,
    back_send,
    back_recv,
    last_send,
    last_recv,
):
    place = Place()
    barrier, count = greet(place)
    partners = [place.other_core()]
    partners += [place.along(axis, step) for axis in "xyz" for step in (1, 2, 3)]
    for partner in partners:
        pl.semaphore_signal(barrier, inc=1, device_id=partner, device_id_type=MESH)
    pl.semaphore_wait(barrier, count + len(partners))

    mine = pl.multiple_of(place.core * 1024, 1024)
    theirs = pl.multiple_of(1024 - place.core * 1024, 1024)
    waits = []

    def send(source, target, send_sem, recv_sem, device):
        copy = pltpu.make_async_remote_copy(
            src_ref=source,
            dst_ref=target,
            send_sem=send_sem,
            recv_sem=recv_sem,
            device_id=device,
            device_id_type=MESH,
        )
        copy.start()
        waits.append(copy)
        return copy

    pair = [
        send(
            gw_ref.at[p, pl.ds(theirs, 1024)],
            pair_ref.at[p],
            pair_send.at[p],
            pair_recv.at[p],
            place.other_core(),
        )
        for p in range(PARTS)
    ]

    strip_first = {-1: 0, 0: 6, 1: 22}
    middle_slot = {-1: 0, 1: 288}
    side_slot = {-1: 0, 0: 144, 1: 528}
    routes = []
    for dlat in (-1, 0, 1):
        rows = 16 if dlat == 0 else 6
        for dlon in (-1, 0, 1):
            first = strip_first[dlat]
            if dlon == 0:
                if dlat == 0:
                    continue
                source = wide_ref.at[pl.ds(48 * first, 48 * rows)]
                target = middle_ref.at[pl.ds(middle_slot[dlat], 48 * rows)]
            else:
                side = OWN if dlon == -1 else OWN + SIDE
                slot = SIDE if dlon == -1 else 0
                source = wide_ref.at[pl.ds(side + 24 * first, 24 * rows)]
                target = sides_ref.at[pl.ds(slot + side_slot[dlat], 24 * rows)]
            routes.append((dlat, dlon, source, target))
    halo = halo_copies(place, halo_send, halo_recv, routes)
    for sends, _, copy in halo:
        guarded(sends, copy.start)

    buffers = ((send0, recv0), (send1, recv1), (send2, recv2))
    pending = [[pair[p]] for p in range(PARTS)]
    base = [0] * PARTS
    for stage in range(3):
        rows = BLOCKS[stage]
        outgoing, incoming = buffers[stage]
        for p in range(PARTS):
            for copy in pending[p]:
                copy.wait_recv()
            if stage == 0:
                acc_ref[p] = gw_ref[p, pl.ds(mine, 1024), :].astype(F32) + pair_ref[p].astype(F32)
            else:
                before = buffers[stage - 1][1]
                here = pl.ds(base[p], BLOCKS[stage - 1])
                total = acc_ref[p, here, :]
                for step in range(3):
                    total = total + before[p, step].astype(F32)
                acc_ref[p, here, :] = total
            axis = ORDERS[p][stage]
            me = place.index(axis)
            pending[p] = []
            for step in (1, 2, 3):
                block = base[p] + lax.rem(me + step, 4) * rows
                block = pl.multiple_of(block, rows)
                outgoing[p, step - 1] = acc_ref[p, pl.ds(block, rows), :].astype(BF16)
                slot = (p * 3 + stage) * 3 + step - 1
                pending[p].append(
                    send(
                        outgoing.at[p, step - 1],
                        incoming.at[p, step - 1],
                        ring_send.at[slot],
                        ring_recv.at[slot],
                        place.along(axis, step),
                    )
                )
            base[p] = pl.multiple_of(base[p] + me * rows, rows)

    for stage in (3, 2, 1, 0):
        for p in range(PARTS):
            for copy in pending[p]:
                copy.wait_recv()
            if stage == 3:
                here = pl.ds(base[p], 16)
                total = acc_ref[p, here, :]
                for step in range(3):
                    total = total + recv2[p, step].astype(F32)
                sum_ref[p, pl.ds(pl.multiple_of(mine + base[p], 16), 16), :] = total.astype(BF16)
            if stage > 0:
                rows = BLOCKS[stage - 1]
                axis = ORDERS[p][stage - 1]
                here = sum_ref.at[p, pl.ds(pl.multiple_of(mine + base[p], rows), rows)]
                pending[p] = []
                for step in (1, 2, 3):
                    slot = (p * 3 + stage - 1) * 3 + step - 1
                    pending[p].append(
                        send(
                            here,
                            here,
                            back_send.at[slot],
                            back_recv.at[slot],
                            place.along(axis, step),
                        )
                    )
                base[p] = base[p] - place.index(axis) * rows
            else:
                here = sum_ref.at[p, pl.ds(mine, 1024)]
                pending[p] = [
                    send(here, here, last_send.at[p], last_recv.at[p], place.other_core())
                ]

    for sends, receives, copy in halo:
        guarded(sends, copy.wait_send)
        guarded(receives, copy.wait_recv)
    for half in range(2):
        part = sides_ref[pl.ds(SIDE * half + 144, 384), :].astype(F32).reshape(48, 8, D)
        own_ref_part = own_ref[:, 8 * half : 8 * half + 8, :]
        acc = own_ref_part + part
        out_ref[:, 8 * half : 8 * half + 8, :] = acc

    def edge(slot, side, first):
        rows = pl.ds(3 * first, 18)
        out_ref[rows] = out_ref[rows] + middle_ref[pl.ds(slot, 288), :].astype(F32).reshape(18, 16, D)
        for half in range(2):
            part = sides_ref[pl.ds(SIDE * half + side, 144), :].astype(F32).reshape(18, 8, D)
            view = out_ref[rows, 8 * half : 8 * half + 8, :]
            out_ref[rows, 8 * half : 8 * half + 8, :] = view + part

    pl.when(place.lat < 7)(lambda: edge(0, 0, 10))
    pl.when(place.lat > 0)(lambda: edge(288, 528, 0))

    for p in range(PARTS):
        pending[p][0].wait_recv()
    for copy in waits:
        copy.wait_send()


def reduce(gt_own, gt_wide, gw):
    vmem = pl.BlockSpec(memory_space=pltpu.VMEM)
    dma = pltpu.SemaphoreType.DMA
    scratch = [
        pltpu.VMEM((576, D), BF16),
        pltpu.VMEM((2 * SIDE, D), BF16),
        pltpu.VMEM((PARTS, 1024, WIDTH), F32),
        pltpu.VMEM((PARTS, 1024, WIDTH), BF16),
    ]
    for rows in BLOCKS:
        scratch += [pltpu.VMEM((PARTS, 3, rows, WIDTH), BF16)] * 2
    for count in (8, PARTS, 9 * PARTS, 9 * PARTS, PARTS):
        scratch += [dma((count,))] * 2
    return pl.pallas_call(
        reduce_kernel,
        out_shape=(
            jax.ShapeDtypeStruct((48, 16, D), F32),
            jax.ShapeDtypeStruct((PARTS, 4 * D, WIDTH), BF16),
        ),
        in_specs=[vmem] * 3,
        out_specs=(vmem,) * 2,
        scratch_shapes=scratch,
        compiler_params=pltpu.CompilerParams(
            collective_id=1, has_side_effects=True, vmem_limit_bytes=40 * 1024 * 1024
        ),
    )(gt_own.reshape(48, 16, D), gt_wide, gw)


def on_device(tokens, w_query, w_key, w_value, w_out, grad_out):
    lat_dev = tokens.shape[0]
    lat_total = lat_dev * lax.axis_size("lat")
    x = tokens.transpose(0, 2, 1, 3).reshape(768, D)
    g = grad_out.transpose(0, 2, 1, 3).reshape(768, D)
    row0 = (lax.axis_index("lat") * lat_dev).astype(jnp.int32).reshape(1)
    wide = gather(x)
    gt_own, gt_wide, gw = attention(row0, wide, g, w_query, w_key, w_value, w_out, lat_total)
    grad_tokens, sums = reduce(gt_own, gt_wide, gw)
    grad_tokens = grad_tokens.reshape(16, 3, 16, D).transpose(0, 2, 1, 3).astype(BF16)
    sums = sums.reshape(PARTS, 4, D, WIDTH).transpose(1, 2, 0, 3).reshape(4, D, D).astype(F32)
    return grad_tokens, sums[0], sums[1], sums[2], sums[3]


def solution(mesh):
    placed = (P("lat", "lon", None, None), P(), P(), P(), P(), P("lat", "lon", None, None))
    return jax.shard_map(
        on_device,
        mesh=mesh,
        in_specs=placed,
        out_specs=(P("lat", "lon", None, None), P(), P(), P(), P()),
        check_vma=False,
    )
```

```python
import jax
import jax.numpy as jnp
from jax import lax
from jax.experimental import pallas as pl
from jax.experimental.pallas import tpu as pltpu
from jax.sharding import PartitionSpec as P

HEADS = 8
HEAD = 64
D = 512
RIM = 6
SPAN = 13
LATITUDES = 128
OWN = 28 * 48
SIDE = 28 * 24
ALL = OWN + 2 * SIDE
TQ = 96
KEYS = 768 + 384
CHUNK = 384
PARTS = 4
WIDTH = D // PARTS
MESH = pl.DeviceIdType.MESH
F32 = jnp.float32
BF16 = jnp.bfloat16


def nn(a, b):
    return jnp.dot(a, b, preferred_element_type=F32)


def nt(a, b):
    return lax.dot_general(a, b, (((1,), (1,)), ((), ())), preferred_element_type=F32)


def tn(a, b):
    return lax.dot_general(a, b, (((0,), (0,)), ((), ())), preferred_element_type=F32)


ORDERS = (("x", "y", "z"), ("y", "z", "x"), ("z", "x", "y"), ("x", "z", "y"))
BLOCKS = (256, 64, 16)


class Place:
    def __init__(self):
        self.lat = lax.axis_index("lat")
        self.lon = lax.axis_index("lon")
        self.z = self.lat % 4
        self.core = self.lon % 2
        self.x = self.lon // 4
        self.y = (self.lat // 4) * 2 + (self.lon // 2) % 2
        self.inside = {-1: self.lat > 0, 0: None, 1: self.lat < 7}

    def near(self, dlat, dlon):
        return (self.lat + dlat, lax.rem(self.lon + dlon + 16, 16))

    def along(self, axis, step):
        x, y, z = self.x, self.y, self.z
        if axis == "x":
            x = lax.rem(x + step, 4)
        elif axis == "y":
            y = lax.rem(y + step, 4)
        else:
            z = lax.rem(z + step, 4)
        return ((y // 2) * 4 + z, x * 4 + (y % 2) * 2 + self.core)

    def other_core(self):
        return (self.lat, self.lon + 1 - 2 * self.core)

    def index(self, axis):
        return {"x": self.x, "y": self.y, "z": self.z}[axis]


def guarded(condition, action):
    if condition is None:
        action()
    else:
        pl.when(condition)(action)


def halo_copies(place, send_sem, recv_sem, routes):
    copies = []
    for i, (dlat, dlon, source, target) in enumerate(routes):
        copy = pltpu.make_async_remote_copy(
            src_ref=source,
            dst_ref=target,
            send_sem=send_sem.at[i],
            recv_sem=recv_sem.at[i],
            device_id=place.near(dlat, dlon),
            device_id_type=MESH,
        )
        copies.append((place.inside[dlat], place.inside[-dlat], copy))
    return copies


def greet(place):
    barrier = pltpu.get_barrier_semaphore()
    for dlat in (-1, 0, 1):
        for dlon in (-1, 0, 1):
            if dlat or dlon:

                def signal(dlat=dlat, dlon=dlon):
                    pl.semaphore_signal(
                        barrier, inc=1, device_id=place.near(dlat, dlon), device_id_type=MESH
                    )

                guarded(place.inside[dlat], signal)
    rows = jnp.where(place.lat > 0, 3, 0) + jnp.where(place.lat < 7, 3, 0)
    return barrier, 2 + rows


def kernel(
    x_hbm,
    grad_hbm,
    wq_hbm,
    wk_hbm,
    wv_hbm,
    wo_hbm,
    out_ref,
    sum_ref,
    tok_ref,
    grad_ref,
    w_ref,
    k_ref,
    v_ref,
    kt_ref,
    vt_ref,
    q_ref,
    u_ref,
    gk_ref,
    gv_ref,
    gq_ref,
    att_ref,
    qbd_ref,
    ubd_ref,
    ubdt_ref,
    bias_ref,
    s_ref,
    p_ref,
    ds_ref,
    gw_ref,
    middle_ref,
    sides_ref,
    pair_ref,
    recv0,
    recv1,
    recv2,
    load_sem,
    gather_send,
    gather_recv,
    halo_send,
    halo_recv,
    pair_send,
    pair_recv,
    ring_send,
    ring_recv,
    back_send,
    back_recv,
    last_send,
    last_recv,
):
    place = Place()
    row0 = place.lat * 16
    wq_ref, wk_ref, wv_ref, wo_ref = [w_ref.at[i] for i in range(4)]
    own_rows = pl.ds(RIM * 48, 768)

    loads = [
        pltpu.make_async_copy(source, target, load_sem.at[i])
        for i, (source, target) in enumerate(
            (
                (x_hbm, tok_ref.at[own_rows]),
                (wk_hbm, wk_ref),
                (wv_hbm, wv_ref),
                (wq_hbm, wq_ref),
                (grad_hbm, grad_ref),
                (wo_hbm, wo_ref),
            )
        )
    ]
    for load in loads:
        load.start()

    barrier, count = greet(place)
    partners = [place.other_core()]
    partners += [place.along(axis, step) for axis in "xyz" for step in (1, 2, 3)]
    for partner in partners:
        pl.semaphore_signal(barrier, inc=1, device_id=partner, device_id_type=MESH)

    loads[0].wait()
    x = tok_ref[own_rows, :].astype(F32).reshape(48, 16, D)
    gw_ref[0:384, :] = x[:, 0:8].reshape(384, D).astype(BF16)
    gw_ref[384:768, :] = x[:, 8:16].reshape(384, D).astype(BF16)
    pl.semaphore_wait(barrier, count + len(partners))

    strip_first = {-1: 22, 0: 6, 1: 0}
    lat_rows = {-1: (0, 6), 0: (0, 16), 1: (10, 6)}
    routes = []
    for dlat in (-1, 0, 1):
        begin, size = lat_rows[dlat]
        for dlon in (-1, 0, 1):
            first = strip_first[dlat]
            if dlon == 0:
                if dlat == 0:
                    continue
                source = tok_ref.at[pl.ds(48 * (RIM + begin), 48 * size)]
                target = tok_ref.at[pl.ds(48 * first, 48 * size)]
            else:
                half = 384 if dlon == 1 else 0
                side = OWN if dlon == 1 else OWN + SIDE
                source = gw_ref.at[pl.ds(half + 24 * begin, 24 * size)]
                target = tok_ref.at[pl.ds(side + 24 * first, 24 * size)]
            routes.append((dlat, dlon, source, target))
    gathered = halo_copies(place, gather_send, gather_recv, routes)
    for sends, _, copy in gathered:
        guarded(sends, copy.start)

    def clear(first):
        tok_ref[pl.ds(48 * first, 288), :] = jnp.zeros((288, D), BF16)
        tok_ref[pl.ds(OWN + 24 * first, 144), :] = jnp.zeros((144, D), BF16)
        tok_ref[pl.ds(OWN + SIDE + 24 * first, 144), :] = jnp.zeros((144, D), BF16)

    pl.when(place.lat == 0)(lambda: clear(0))
    pl.when(place.lat == 7)(lambda: clear(22))

    def project(rows):
        x = tok_ref[rows, :]
        k_ref[rows, :] = nn(x, wk_ref[...]).astype(BF16)
        v_ref[rows, :] = nn(x, wv_ref[...]).astype(BF16)

    loads[1].wait()
    loads[2].wait()
    project(own_rows)
    loads[3].wait()
    q = nn(tok_ref[own_rows, :], wq_ref[...]).astype(BF16).astype(F32) * 0.125
    q_ref[...] = q.reshape(48, 16, D)
    loads[4].wait()
    loads[5].wait()
    u = nt(grad_ref[...], wo_ref[...]).astype(BF16).astype(F32)
    u_ref[...] = u.reshape(48, 16, D)

    def zero(i, carry):
        rows = pl.ds(pl.multiple_of(i * 168, 168), 168)
        gk_ref[rows, :] = jnp.zeros((168, D), F32)
        gv_ref[rows, :] = jnp.zeros((168, D), F32)
        return carry

    lax.fori_loop(0, ALL // 168, zero, 0)

    head_row = lax.broadcasted_iota(jnp.int32, (256, 256), 0)
    feature = lax.broadcasted_iota(jnp.int32, (256, 256), 1)

    def diagonal(n):
        owner = (head_row + 256 * n) // TQ
        return owner == (feature + 128 * n) // HEAD

    def band_start(r):
        lowest = jnp.where(place.lat == 0, RIM, 0)
        highest = jnp.where(place.lat == 7, RIM, 12)
        return jnp.minimum(jnp.maximum(4 * r, lowest), highest)

    def fill_bias(r):
        base = band_start(r)
        lane = lax.broadcasted_iota(jnp.int32, (1, 384), 1) % TQ
        q_lat = row0 + 4 * r + lane // 24
        first = jnp.clip(q_lat - RIM, 0, LATITUDES - SPAN) - (row0 + base - RIM)
        q_col = lane % 8

        def bias(d_lat, d_col):
            inside = (d_lat >= 0) & (d_lat < SPAN) & (d_col >= 0) & (d_col < SPAN)
            return jnp.where(inside, 0.0, -jnp.inf)

        for c in range(2):
            key = lax.broadcasted_iota(jnp.int32, (768, 1), 0)
            rows = pl.ds(CHUNK * (1 - c), 768)
            bias_ref[c, rows, :] = bias(key // 48 - first, key % 16 - 8 * c - q_col + RIM)
            key = lax.broadcasted_iota(jnp.int32, (384, 1), 0)
            rows = pl.ds(768 * c, 384)
            bias_ref[c, rows, :] = bias(key // 24 - first, key % 8 + (16 * c - 8) - q_col + RIM)

    fill_bias(0)

    for sends, receives, copy in gathered:
        guarded(sends, copy.wait_send)
        guarded(receives, copy.wait_recv)
    project(pl.ds(0, 288))
    project(pl.ds(1056, 288))
    project(pl.ds(OWN, SIDE))
    project(pl.ds(OWN + SIDE, SIDE))

    def latitude_band(r, carry):
        base = band_start(r)
        north = (place.lat == 0) & ((r == 1) | (r == 2))
        south = (place.lat == 7) & (r >= 2)
        pl.when(north | south)(lambda: fill_bias(r))
        own = [pl.multiple_of(base * 48 + 384 * i, 48) for i in range(2)]
        side = [pl.multiple_of(OWN + SIDE * c + base * 24, 48) for c in range(2)]
        for i, start in enumerate((side[0], own[0], own[1], side[1])):
            part = pl.ds(start, CHUNK)
            kt_ref[:, pl.ds(CHUNK * i, CHUNK)] = k_ref[part, :].T
            vt_ref[:, pl.ds(CHUNK * i, CHUNK)] = v_ref[part, :].T
        starts = ((side[0], own[0], own[1]), (own[0], own[1], side[1]))
        groups = pl.ds(12 * r, 12)

        for c in range(2):
            q_tile = q_ref[groups, 8 * c : 8 * c + 8, :].reshape(TQ, D).astype(BF16)
            u_tile = u_ref[groups, 8 * c : 8 * c + 8, :].reshape(TQ, D).astype(BF16)
            q_all = jnp.concatenate([q_tile] * HEADS, axis=0)
            u_all = jnp.concatenate([u_tile] * HEADS, axis=0)
            for n in range(3):
                keep = diagonal(n)
                block = q_all[256 * n : 256 * n + 256, 128 * n : 128 * n + 256]
                qbd_ref[3 * c + n] = jnp.where(keep, block, jnp.zeros_like(block))
                block = u_all[256 * n : 256 * n + 256, 128 * n : 128 * n + 256]
                block = jnp.where(keep, block, jnp.zeros_like(block))
                ubd_ref[3 * c + n] = block
                ubdt_ref[3 * c + n] = block.T
            att_ref[groups, 8 * c : 8 * c + 8, :] = jnp.zeros((12, 8, D), F32)
            gq_ref[groups, 8 * c : 8 * c + 8, :] = jnp.zeros((12, 8, D), F32)

        def fold(ref, c, n, block):
            block = jnp.where(diagonal(n), block, 0.0)
            row = 256 * n
            while row < 256 * n + 256:
                h = row // TQ
                end = min(TQ * (h + 1), 256 * n + 256)
                begin = row - TQ * h
                count = (end - row) // 8
                view = (
                    pl.ds(12 * r + begin // 8, count),
                    slice(8 * c, 8 * c + 8),
                    slice(128 * n, 128 * n + 256),
                )
                ref[view] += block[row - 256 * n : end - 256 * n].reshape(count, 8, 256)
                row = end

        state = [{} for _ in range(6)]

        def parts(b):
            return b // 3, b % 3, pl.ds(128 * (b % 3), 256)

        def score(b):
            c, n, feats = parts(b)
            bias_lanes = ((0, 128), (256, 0), (128, 256))[n]
            high = jnp.full((8, 256), -jnp.inf, F32)
            for j in range(3):
                part = pl.ds(CHUNK * j, CHUNK)
                x = nt(k_ref[pl.ds(starts[c][j], CHUNK), feats], qbd_ref[b])
                x = x + jnp.concatenate(
                    [bias_ref[c, part, pl.ds(lane, 128)] for lane in bias_lanes], axis=1
                )
                s_ref[b % 4, part, :] = x
                high = jnp.maximum(high, jnp.max(x.reshape(CHUNK // 8, 8, 256), axis=0))
                yield
            state[b]["high"] = jnp.max(high, axis=0, keepdims=True)

        def exponent(b):
            high = state[b]["high"]
            total = jnp.zeros((8, 256), F32)
            for j in range(3):
                part = pl.ds(CHUNK * j, CHUNK)
                e = jnp.exp(s_ref[b % 4, part, :] - high)
                s_ref[b % 4, part, :] = e
                total = total + jnp.sum(e.reshape(CHUNK // 8, 8, 256), axis=0)
                yield
            state[b]["scale"] = 1.0 / jnp.sum(total, axis=0, keepdims=True)

        def attend(b):
            c, n, feats = parts(b)
            scale = state[b]["scale"]
            for j in range(3):
                part = pl.ds(CHUNK * j, CHUNK)
                p = s_ref[b % 4, part, :] * scale
                s_ref[b % 4, part, :] = p
                p_ref[b % 2, part, :] = p.astype(BF16)
                yield
            out_t = nn(vt_ref[feats, pl.ds(CHUNK * c, KEYS)], p_ref[b % 2])
            out_t = out_t.astype(BF16).astype(F32)
            state[b]["row_dot"] = jnp.sum(out_t * ubdt_ref[b].astype(F32), axis=0, keepdims=True)
            fold(att_ref, c, n, out_t.T)

        def gradient(b):
            c, n, feats = parts(b)
            row_dot = state[b]["row_dot"]
            for j in range(3):
                part = pl.ds(CHUNK * j, CHUNK)
                rows = pl.ds(starts[c][j], CHUNK)
                grad_p = nt(v_ref[rows, feats], ubd_ref[b])
                ds = (s_ref[b % 4, part, :] * (grad_p - row_dot)).astype(BF16)
                ds_ref[part, :] = ds
                gv_ref[rows, feats] += nn(p_ref[b % 2, part, :], ubd_ref[b])
                gk_ref[rows, feats] += nn(ds, qbd_ref[b])
                yield
            gq_t = nn(kt_ref[feats, pl.ds(CHUNK * c, KEYS)], ds_ref[...])
            fold(gq_ref, c, n, gq_t.T)

        stages = (score, exponent, attend, gradient)
        for step in range(6 + len(stages) - 1):
            running = [
                stage(step - i) for i, stage in enumerate(stages) if 0 <= step - i < 6
            ]
            while running:
                running = [g for g in running if next(g, running) is None]
        return carry

    lax.fori_loop(0, 4, latitude_band, 0)

    def send(source, target, send_sem, recv_sem, device):
        copy = pltpu.make_async_remote_copy(
            src_ref=source,
            dst_ref=target,
            send_sem=send_sem,
            recv_sem=recv_sem,
            device_id=device,
            device_id_type=MESH,
        )
        copy.start()
        waits.append(copy)
        return copy

    waits = []

    def to_tokens(rows):
        gk_low = gk_ref[rows, :].astype(BF16)
        gv_low = gv_ref[rows, :].astype(BF16)
        return nt(gk_low, wk_ref[...]) + nt(gv_low, wv_ref[...])

    for rows in (pl.ds(OWN, SIDE), pl.ds(OWN + SIDE, SIDE), pl.ds(0, 288), pl.ds(1056, 288)):
        k_ref[rows, :] = to_tokens(rows).astype(BF16)
    strip_first = {-1: 0, 0: 6, 1: 22}
    middle_slot = {-1: 0, 1: 288}
    side_slot = {-1: 0, 0: 144, 1: 528}
    routes = []
    for dlat in (-1, 0, 1):
        size = 16 if dlat == 0 else 6
        for dlon in (-1, 0, 1):
            first = strip_first[dlat]
            if dlon == 0:
                if dlat == 0:
                    continue
                source = k_ref.at[pl.ds(48 * first, 48 * size)]
                target = middle_ref.at[pl.ds(middle_slot[dlat], 48 * size)]
            else:
                side = OWN if dlon == -1 else OWN + SIDE
                slot = SIDE if dlon == -1 else 0
                source = k_ref.at[pl.ds(side + 24 * first, 24 * size)]
                target = sides_ref.at[pl.ds(slot + side_slot[dlat], 24 * size)]
            routes.append((dlat, dlon, source, target))
    halo = halo_copies(place, halo_send, halo_recv, routes)
    for sends, _, copy in halo:
        guarded(sends, copy.start)

    gq_low = (gq_ref[...].reshape(768, D) * 0.125).astype(BF16)
    core = place.core
    pieces = (
        (core * 1536, 1536 - core * 1536, core * 512),
        (512 + core * 512, 1024 - core * 512, 512 - core * 512),
    )

    def exchange(piece):
        theirs = pl.multiple_of(pieces[piece][1], 512)
        copies = []
        for p in range(PARTS):
            columns = pl.ds(WIDTH * p, WIDTH)
            copies.append(
                send(
                    gw_ref.at[pl.ds(theirs, 512), columns],
                    pair_ref.at[piece, :, columns],
                    pair_send.at[PARTS * piece + p],
                    pair_recv.at[PARTS * piece + p],
                    place.other_core(),
                )
            )
        return copies

    gw_ref[pl.ds(0, D), :] = tn(tok_ref[own_rows, :], gq_low).astype(BF16)
    att_low = att_ref[...].reshape(768, D).astype(BF16)
    gw_ref[pl.ds(3 * D, D), :] = tn(att_low, grad_ref[...]).astype(BF16)
    first_pair = exchange(0)
    gw_ref[pl.ds(D, D), :] = tn(tok_ref[...], gk_ref[...].astype(BF16)).astype(BF16)
    gw_ref[pl.ds(2 * D, D), :] = tn(tok_ref[...], gv_ref[...].astype(BF16)).astype(BF16)
    second_pair = exchange(1)
    own = to_tokens(own_rows) + nt(gq_low, wq_ref[...])
    q_ref[...] = own.reshape(48, 16, D)

    mine = pl.multiple_of(core * 1024, 1024)
    acc_lanes = pl.ds(0, WIDTH)
    buffers = (recv0, recv1, recv2)
    staged = (0, 768, 960)
    pending = [[first_pair[p], second_pair[p]] for p in range(PARTS)]
    base = [0] * PARTS
    for stage in range(3):
        rows = BLOCKS[stage]
        incoming = buffers[stage]
        for p in range(PARTS):
            for copy in pending[p]:
                copy.wait_recv()
            if stage == 0:
                columns = pl.ds(WIDTH * p, WIDTH)
                for piece in range(2):
                    source, _, target = pieces[piece]
                    here = pl.ds(pl.multiple_of(source, 512), 512)
                    total = gw_ref[here, columns].astype(F32)
                    total = total + pair_ref[piece, :, columns].astype(F32)
                    s_ref[p, pl.ds(pl.multiple_of(target, 512), 512), acc_lanes] = total
            else:
                before = buffers[stage - 1]
                here = pl.ds(base[p], BLOCKS[stage - 1])
                total = s_ref[p, here, acc_lanes]
                for step in range(3):
                    total = total + before[p, step].astype(F32)
                s_ref[p, here, acc_lanes] = total
            axis = ORDERS[p][stage]
            me = place.index(axis)
            pending[p] = []
            for step in (1, 2, 3):
                block = base[p] + lax.rem(me + step, 4) * rows
                block = pl.multiple_of(block, rows)
                outgoing = p_ref.at[
                    p // 2,
                    pl.ds(staged[stage] + rows * (step - 1), rows),
                    pl.ds(WIDTH * (p % 2), WIDTH),
                ]
                outgoing[...] = s_ref[p, pl.ds(block, rows), acc_lanes].astype(BF16)
                slot = (p * 3 + stage) * 3 + step - 1
                pending[p].append(
                    send(
                        outgoing,
                        incoming.at[p, step - 1],
                        ring_send.at[slot],
                        ring_recv.at[slot],
                        place.along(axis, step),
                    )
                )
            base[p] = pl.multiple_of(base[p] + me * rows, rows)

    for stage in (3, 2, 1, 0):
        for p in range(PARTS):
            columns = pl.ds(WIDTH * p, WIDTH)
            for copy in pending[p]:
                copy.wait_recv()
            if stage == 3:
                total = s_ref[p, pl.ds(base[p], 16), acc_lanes]
                for step in range(3):
                    total = total + recv2[p, step].astype(F32)
                here = pl.ds(pl.multiple_of(mine + base[p], 16), 16)
                sum_ref[here, columns] = total.astype(BF16)
            if stage > 0:
                rows = BLOCKS[stage - 1]
                axis = ORDERS[p][stage - 1]
                here = pl.ds(pl.multiple_of(mine + base[p], rows), rows)
                here = sum_ref.at[here, columns]
                pending[p] = []
                for step in (1, 2, 3):
                    slot = (p * 3 + stage - 1) * 3 + step - 1
                    pending[p].append(
                        send(
                            here,
                            here,
                            back_send.at[slot],
                            back_recv.at[slot],
                            place.along(axis, step),
                        )
                    )
                base[p] = base[p] - place.index(axis) * rows
            else:
                here = sum_ref.at[pl.ds(mine, 1024), columns]
                pending[p] = [
                    send(here, here, last_send.at[p], last_recv.at[p], place.other_core())
                ]

    for sends, receives, copy in halo:
        guarded(sends, copy.wait_send)
        guarded(receives, copy.wait_recv)
    for half in range(2):
        part = sides_ref[pl.ds(SIDE * half + 144, 384), :].astype(F32).reshape(48, 8, D)
        view = q_ref[:, 8 * half : 8 * half + 8, :]
        q_ref[:, 8 * half : 8 * half + 8, :] = view + part

    def edge(slot, side, first):
        rows = pl.ds(3 * first, 18)
        part = middle_ref[pl.ds(slot, 288), :].astype(F32).reshape(18, 16, D)
        q_ref[rows] = q_ref[rows] + part
        for half in range(2):
            part = sides_ref[pl.ds(SIDE * half + side, 144), :].astype(F32).reshape(18, 8, D)
            view = q_ref[rows, 8 * half : 8 * half + 8, :]
            q_ref[rows, 8 * half : 8 * half + 8, :] = view + part

    pl.when(place.lat < 7)(lambda: edge(0, 0, 10))
    pl.when(place.lat > 0)(lambda: edge(288, 528, 0))
    out_ref[...] = q_ref[...].reshape(768, D).astype(BF16)

    for p in range(PARTS):
        pending[p][0].wait_recv()
    for copy in waits:
        copy.wait_send()


def whole(x, g, w_query, w_key, w_value, w_out):
    dma = pltpu.SemaphoreType.DMA
    shapes = [
        ((ALL, D), BF16),
        ((768, D), BF16),
        ((4, D, D), BF16),
        ((ALL, D), BF16),
        ((ALL, D), BF16),
        ((D, 1536), BF16),
        ((D, 1536), BF16),
        ((48, 16, D), F32),
        ((48, 16, D), F32),
        ((ALL, D), F32),
        ((ALL, D), F32),
        ((48, 16, D), F32),
        ((48, 16, D), F32),
        ((6, 256, 256), BF16),
        ((6, 256, 256), BF16),
        ((6, 256, 256), BF16),
        ((2, KEYS, 384), F32),
        ((4, KEYS, 256), F32),
        ((2, KEYS, 256), BF16),
        ((KEYS, 256), BF16),
        ((4 * D, D), BF16),
        ((576, D), BF16),
        ((2 * SIDE, D), BF16),
        ((2, D, D), BF16),
    ]
    for rows in BLOCKS:
        shapes.append(((PARTS, 3, rows, WIDTH), BF16))
    scratch = [pltpu.VMEM(shape, kind) for shape, kind in shapes]
    scratch.append(dma((6,)))
    for count in (8, 8, 2 * PARTS, 9 * PARTS, 9 * PARTS, PARTS):
        scratch += [dma((count,))] * 2
    return pl.pallas_call(
        kernel,
        out_shape=(
            jax.ShapeDtypeStruct((768, D), BF16),
            jax.ShapeDtypeStruct((4 * D, D), BF16),
        ),
        in_specs=[pl.BlockSpec(memory_space=pl.ANY)] * 6,
        out_specs=(pl.BlockSpec(memory_space=pltpu.VMEM),) * 2,
        scratch_shapes=scratch,
        compiler_params=pltpu.CompilerParams(
            collective_id=0, has_side_effects=True, vmem_limit_bytes=62 * 1024 * 1024
        ),
    )(x, g, w_query, w_key, w_value, w_out)


def on_device(tokens, w_query, w_key, w_value, w_out, grad_out):
    x = tokens.transpose(0, 2, 1, 3).reshape(768, D)
    g = grad_out.transpose(0, 2, 1, 3).reshape(768, D)
    grad_tokens, sums = whole(x, g, w_query, w_key, w_value, w_out)
    grad_tokens = grad_tokens.reshape(16, 3, 16, D).transpose(0, 2, 1, 3)
    sums = sums.reshape(4, D, D).astype(F32)
    return grad_tokens, sums[0], sums[1], sums[2], sums[3]


def solution(mesh):
    placed = (P("lat", "lon", None, None), P(), P(), P(), P(), P("lat", "lon", None, None))
    return jax.shard_map(
        on_device,
        mesh=mesh,
        in_specs=placed,
        out_specs=(P("lat", "lon", None, None), P(), P(), P(), P()),
        check_vma=False,
    )
```

```python
import jax
import jax.numpy as jnp
from jax import lax
from jax.experimental import pallas as pl
from jax.experimental.pallas import tpu as pltpu
from jax.sharding import PartitionSpec as P

HEADS = 8
HEAD = 64
D = 512
RIM = 6
SPAN = 13
LATITUDES = 128
OWN = 28 * 48
SIDE = 28 * 24
ALL = OWN + 2 * SIDE
TQ = 96
KEYS = 768 + 384
CHUNK = 384
PARTS = 4
WIDTH = D // PARTS
MESH = pl.DeviceIdType.MESH
F32 = jnp.float32
BF16 = jnp.bfloat16


def nn(a, b):
    return jnp.dot(a, b, preferred_element_type=F32)


def nt(a, b):
    return lax.dot_general(a, b, (((1,), (1,)), ((), ())), preferred_element_type=F32)


def tn(a, b):
    return lax.dot_general(a, b, (((0,), (0,)), ((), ())), preferred_element_type=F32)


ORDERS = (("x", "z", "y"), ("z", "x", "y"), ("x", "y", "z"), ("z", "y", "x"))
BLOCKS = (256, 64, 16)


class Place:
    def __init__(self):
        self.lat = lax.axis_index("lat")
        self.lon = lax.axis_index("lon")
        self.z = self.lat % 4
        self.core = self.lon % 2
        self.x = self.lon // 4
        self.y = (self.lat // 4) * 2 + (self.lon // 2) % 2
        self.inside = {-1: self.lat > 0, 0: None, 1: self.lat < 7}

    def near(self, dlat, dlon):
        return (self.lat + dlat, lax.rem(self.lon + dlon + 16, 16))

    def along(self, axis, step):
        x, y, z = self.x, self.y, self.z
        if axis == "x":
            x = lax.rem(x + step, 4)
        elif axis == "y":
            y = lax.rem(y + step, 4)
        else:
            z = lax.rem(z + step, 4)
        return ((y // 2) * 4 + z, x * 4 + (y % 2) * 2 + self.core)

    def other_core(self):
        return (self.lat, self.lon + 1 - 2 * self.core)

    def index(self, axis):
        return {"x": self.x, "y": self.y, "z": self.z}[axis]


def guarded(condition, action):
    if condition is None:
        action()
    else:
        pl.when(condition)(action)


def halo_copies(place, send_sem, recv_sem, routes):
    copies = []
    for i, (dlat, dlon, source, target) in enumerate(routes):
        copy = pltpu.make_async_remote_copy(
            src_ref=source,
            dst_ref=target,
            send_sem=send_sem.at[i],
            recv_sem=recv_sem.at[i],
            device_id=place.near(dlat, dlon),
            device_id_type=MESH,
        )
        copies.append((dlat, place.inside[dlat], copy))
    return copies


def greet(place):
    barrier = pltpu.get_barrier_semaphore()
    for dlat in (-1, 0, 1):
        for dlon in (-1, 0, 1):
            if dlat or dlon:

                def signal(dlat=dlat, dlon=dlon):
                    pl.semaphore_signal(
                        barrier, inc=1, device_id=place.near(dlat, dlon), device_id_type=MESH
                    )

                guarded(place.inside[dlat], signal)
    rows = jnp.where(place.lat > 0, 3, 0) + jnp.where(place.lat < 7, 3, 0)
    return barrier, 2 + rows


def kernel(
    x_hbm,
    grad_hbm,
    wq_hbm,
    wk_hbm,
    wv_hbm,
    wo_hbm,
    out_ref,
    sum_ref,
    tok_ref,
    grad_ref,
    w_ref,
    k_ref,
    v_ref,
    kt_ref,
    vt_ref,
    q_ref,
    u_ref,
    gk_ref,
    gv_ref,
    gq_ref,
    att_ref,
    qbd_ref,
    ubd_ref,
    ubdt_ref,
    bias_ref,
    s_ref,
    p_ref,
    ds_ref,
    gw_ref,
    middle_ref,
    sides_ref,
    pair_ref,
    recv0,
    recv1,
    recv2,
    load_sem,
    gather_send,
    gather_recv,
    halo_send,
    halo_recv,
    pair_send,
    pair_recv,
    ring_send,
    ring_recv,
    back_send,
    back_recv,
    last_send,
    last_recv,
):
    place = Place()
    row0 = place.lat * 16
    wq_ref, wk_ref, wv_ref, wo_ref = [w_ref.at[i] for i in range(4)]
    own_rows = pl.ds(RIM * 48, 768)

    loads = [
        pltpu.make_async_copy(source, target, load_sem.at[i])
        for i, (source, target) in enumerate(
            (
                (x_hbm, tok_ref.at[own_rows]),
                (wk_hbm, wk_ref),
                (wv_hbm, wv_ref),
                (wq_hbm, wq_ref),
                (grad_hbm, grad_ref),
                (wo_hbm, wo_ref),
            )
        )
    ]
    for load in loads:
        load.start()

    barrier, count = greet(place)
    partners = [place.other_core()]
    partners += [place.along(axis, step) for axis in "xyz" for step in (1, 2, 3)]
    for partner in partners:
        pl.semaphore_signal(barrier, inc=1, device_id=partner, device_id_type=MESH)

    loads[0].wait()
    x = tok_ref[own_rows, :].astype(F32).reshape(48, 16, D)
    gw_ref[0:384, :] = x[:, 0:8].reshape(384, D).astype(BF16)
    gw_ref[384:768, :] = x[:, 8:16].reshape(384, D).astype(BF16)
    pl.semaphore_wait(barrier, count + len(partners))

    strip_first = {-1: 22, 0: 6, 1: 0}
    lat_rows = {-1: (0, 6), 0: (0, 16), 1: (10, 6)}
    routes = []
    for dlat in (-1, 0, 1):
        begin, size = lat_rows[dlat]
        for dlon in (-1, 0, 1):
            first = strip_first[dlat]
            if dlon == 0:
                if dlat == 0:
                    continue
                source = tok_ref.at[pl.ds(48 * (RIM + begin), 48 * size)]
                target = tok_ref.at[pl.ds(48 * first, 48 * size)]
            else:
                half = 384 if dlon == 1 else 0
                side = OWN if dlon == 1 else OWN + SIDE
                source = gw_ref.at[pl.ds(half + 24 * begin, 24 * size)]
                target = tok_ref.at[pl.ds(side + 24 * first, 24 * size)]
            routes.append((dlat, dlon, source, target))
    gathered = halo_copies(place, gather_send, gather_recv, routes)
    for dlat, sends, copy in gathered:
        guarded(sends, copy.start)

    def clear(first):
        tok_ref[pl.ds(48 * first, 288), :] = jnp.zeros((288, D), BF16)
        tok_ref[pl.ds(OWN + 24 * first, 144), :] = jnp.zeros((144, D), BF16)
        tok_ref[pl.ds(OWN + SIDE + 24 * first, 144), :] = jnp.zeros((144, D), BF16)

    pl.when(place.lat == 0)(lambda: clear(0))
    pl.when(place.lat == 7)(lambda: clear(22))

    def project(rows):
        x = tok_ref[rows, :]
        k_ref[rows, :] = nn(x, wk_ref[...]).astype(BF16)
        v_ref[rows, :] = nn(x, wv_ref[...]).astype(BF16)

    loads[1].wait()
    loads[2].wait()
    project(own_rows)
    loads[3].wait()
    q = nn(tok_ref[own_rows, :], wq_ref[...]).astype(BF16).astype(F32) * 0.125
    q_ref[...] = q.reshape(48, 16, D)
    loads[4].wait()
    loads[5].wait()
    u = nt(grad_ref[...], wo_ref[...]).astype(BF16).astype(F32)
    u_ref[...] = u.reshape(48, 16, D)

    def zero(i, carry):
        rows = pl.ds(pl.multiple_of(i * 168, 168), 168)
        gk_ref[rows, :] = jnp.zeros((168, D), F32)
        gv_ref[rows, :] = jnp.zeros((168, D), F32)
        return carry

    lax.fori_loop(0, ALL // 168, zero, 0)

    head_row = lax.broadcasted_iota(jnp.int32, (256, 256), 0)
    feature = lax.broadcasted_iota(jnp.int32, (256, 256), 1)

    def diagonal(n):
        owner = (head_row + 256 * n) // TQ
        return owner == (feature + 128 * n) // HEAD

    def band_start(r):
        lowest = jnp.where(place.lat == 0, RIM, 0)
        highest = jnp.where(place.lat == 7, RIM, 12)
        return jnp.minimum(jnp.maximum(4 * r, lowest), highest)

    def fill_bias(r):
        base = band_start(r)
        lane = lax.broadcasted_iota(jnp.int32, (1, 384), 1) % TQ
        q_lat = row0 + 4 * r + lane // 24
        first = jnp.clip(q_lat - RIM, 0, LATITUDES - SPAN) - (row0 + base - RIM)
        q_col = lane % 8

        def bias(d_lat, d_col):
            inside = (d_lat >= 0) & (d_lat < SPAN) & (d_col >= 0) & (d_col < SPAN)
            return jnp.where(inside, 0.0, -jnp.inf)

        for c in range(2):
            key = lax.broadcasted_iota(jnp.int32, (768, 1), 0)
            rows = pl.ds(CHUNK * (1 - c), 768)
            bias_ref[c, rows, :] = bias(key // 48 - first, key % 16 - 8 * c - q_col + RIM)
            key = lax.broadcasted_iota(jnp.int32, (384, 1), 0)
            rows = pl.ds(768 * c, 384)
            bias_ref[c, rows, :] = bias(key // 24 - first, key % 8 + (16 * c - 8) - q_col + RIM)

    fill_bias(jnp.where(place.lat < 4, 0, 3))

    upward = place.lat < 4
    for dlat, _, copy in gathered:
        if dlat == 0:
            copy.wait_recv()
        elif dlat == 1:
            pl.when(upward & (place.lat > 0))(copy.wait_recv)
        else:
            pl.when((place.lat >= 4) & (place.lat < 7))(copy.wait_recv)
    project(pl.ds(pl.multiple_of(jnp.where(upward, 0, 1056), 96), 288))
    for side in (OWN, OWN + SIDE):
        project(pl.ds(pl.multiple_of(side + jnp.where(upward, 0, 144), 48), 528))

    def late_halo():
        for dlat, _, copy in gathered:
            if dlat == 1:
                pl.when(place.lat >= 4)(copy.wait_recv)
            elif dlat == -1:
                pl.when(upward)(copy.wait_recv)
        project(pl.ds(pl.multiple_of(jnp.where(upward, 1056, 0), 96), 288))
        for side in (OWN, OWN + SIDE):
            project(pl.ds(pl.multiple_of(side + jnp.where(upward, 528, 0), 48), 144))

    def latitude_band(i, carry):
        r = jnp.where(upward, i, 3 - i)
        base = band_start(r)
        pole = (place.lat == 0) | (place.lat == 7)
        pl.when(pole & ((i == 1) | (i == 2)))(lambda: fill_bias(r))
        pl.when(i == 2)(late_halo)
        own = [pl.multiple_of(base * 48 + 384 * i, 48) for i in range(2)]
        side = [pl.multiple_of(OWN + SIDE * c + base * 24, 48) for c in range(2)]
        for i, start in enumerate((side[0], own[0], own[1], side[1])):
            part = pl.ds(start, CHUNK)
            kt_ref[:, pl.ds(CHUNK * i, CHUNK)] = k_ref[part, :].T
            vt_ref[:, pl.ds(CHUNK * i, CHUNK)] = v_ref[part, :].T
        starts = ((side[0], own[0], own[1]), (own[0], own[1], side[1]))
        groups = pl.ds(12 * r, 12)

        for c in range(2):
            q_tile = q_ref[groups, 8 * c : 8 * c + 8, :].reshape(TQ, D).astype(BF16)
            u_tile = u_ref[groups, 8 * c : 8 * c + 8, :].reshape(TQ, D).astype(BF16)
            q_all = jnp.concatenate([q_tile] * HEADS, axis=0)
            u_all = jnp.concatenate([u_tile] * HEADS, axis=0)
            for n in range(3):
                keep = diagonal(n)
                block = q_all[256 * n : 256 * n + 256, 128 * n : 128 * n + 256]
                qbd_ref[3 * c + n] = jnp.where(keep, block, jnp.zeros_like(block))
                block = u_all[256 * n : 256 * n + 256, 128 * n : 128 * n + 256]
                block = jnp.where(keep, block, jnp.zeros_like(block))
                ubd_ref[3 * c + n] = block
                ubdt_ref[3 * c + n] = block.T
            att_ref[groups, 8 * c : 8 * c + 8, :] = jnp.zeros((12, 8, D), F32)
            gq_ref[groups, 8 * c : 8 * c + 8, :] = jnp.zeros((12, 8, D), F32)

        def fold(ref, c, n, block):
            block = jnp.where(diagonal(n), block, 0.0)
            row = 256 * n
            while row < 256 * n + 256:
                h = row // TQ
                end = min(TQ * (h + 1), 256 * n + 256)
                begin = row - TQ * h
                count = (end - row) // 8
                view = (
                    pl.ds(12 * r + begin // 8, count),
                    slice(8 * c, 8 * c + 8),
                    slice(128 * n, 128 * n + 256),
                )
                ref[view] += block[row - 256 * n : end - 256 * n].reshape(count, 8, 256)
                row = end

        state = [{} for _ in range(6)]

        def parts(b):
            return b // 3, b % 3, pl.ds(128 * (b % 3), 256)

        def score(b):
            c, n, feats = parts(b)
            bias_lanes = ((0, 128), (256, 0), (128, 256))[n]
            high = jnp.full((8, 256), -jnp.inf, F32)
            for j in range(3):
                part = pl.ds(CHUNK * j, CHUNK)
                x = nt(k_ref[pl.ds(starts[c][j], CHUNK), feats], qbd_ref[b])
                x = x + jnp.concatenate(
                    [bias_ref[c, part, pl.ds(lane, 128)] for lane in bias_lanes], axis=1
                )
                s_ref[b % 4, part, :] = x
                high = jnp.maximum(high, jnp.max(x.reshape(CHUNK // 8, 8, 256), axis=0))
                yield
            state[b]["high"] = jnp.max(high, axis=0, keepdims=True)

        def exponent(b):
            high = state[b]["high"]
            total = jnp.zeros((8, 256), F32)
            for j in range(3):
                part = pl.ds(CHUNK * j, CHUNK)
                e = jnp.exp(s_ref[b % 4, part, :] - high)
                s_ref[b % 4, part, :] = e
                total = total + jnp.sum(e.reshape(CHUNK // 8, 8, 256), axis=0)
                yield
            state[b]["scale"] = 1.0 / jnp.sum(total, axis=0, keepdims=True)

        def attend(b):
            c, n, feats = parts(b)
            scale = state[b]["scale"]
            for j in range(3):
                part = pl.ds(CHUNK * j, CHUNK)
                p = s_ref[b % 4, part, :] * scale
                s_ref[b % 4, part, :] = p
                p_ref[b % 2, part, :] = p.astype(BF16)
                yield
            out_t = nn(vt_ref[feats, pl.ds(CHUNK * c, KEYS)], p_ref[b % 2])
            out_t = out_t.astype(BF16).astype(F32)
            state[b]["row_dot"] = jnp.sum(out_t * ubdt_ref[b].astype(F32), axis=0, keepdims=True)
            fold(att_ref, c, n, out_t.T)

        def gradient(b):
            c, n, feats = parts(b)
            row_dot = state[b]["row_dot"]
            for j in range(3):
                part = pl.ds(CHUNK * j, CHUNK)
                rows = pl.ds(starts[c][j], CHUNK)
                grad_p = nt(v_ref[rows, feats], ubd_ref[b])
                ds = (s_ref[b % 4, part, :] * (grad_p - row_dot)).astype(BF16)
                ds_ref[part, :] = ds
                gv_ref[rows, feats] += nn(p_ref[b % 2, part, :], ubd_ref[b])
                gk_ref[rows, feats] += nn(ds, qbd_ref[b])
                yield
            gq_t = nn(kt_ref[feats, pl.ds(CHUNK * c, KEYS)], ds_ref[...])
            fold(gq_ref, c, n, gq_t.T)

        stages = (score, exponent, attend, gradient)
        for step in range(6 + len(stages) - 1):
            running = [
                stage(step - i) for i, stage in enumerate(stages) if 0 <= step - i < 6
            ]
            while running:
                running = [g for g in running if next(g, running) is None]
        return carry

    lax.fori_loop(0, 4, latitude_band, 0)

    def send(source, target, send_sem, recv_sem, device):
        copy = pltpu.make_async_remote_copy(
            src_ref=source,
            dst_ref=target,
            send_sem=send_sem,
            recv_sem=recv_sem,
            device_id=device,
            device_id_type=MESH,
        )
        copy.start()
        waits.append(copy)
        return copy

    waits = []

    def to_tokens(rows):
        gk_low = gk_ref[rows, :].astype(BF16)
        gv_low = gv_ref[rows, :].astype(BF16)
        return nt(gk_low, wk_ref[...]) + nt(gv_low, wv_ref[...])

    for dlat, sends, copy in gathered:
        guarded(sends, copy.wait_send)
    along_lon = []
    for i, (dlon, source, target) in enumerate(((-1, OWN, SIDE), (1, OWN + SIDE, 0))):
        k_ref[pl.ds(source, SIDE), :] = to_tokens(pl.ds(source, SIDE)).astype(BF16)
        along_lon.append(
            send(
                k_ref.at[pl.ds(source, SIDE)],
                sides_ref.at[pl.ds(target, SIDE)],
                halo_send.at[i],
                halo_recv.at[i],
                place.near(0, dlon),
            )
        )

    gq_low = (gq_ref[...].reshape(768, D) * 0.125).astype(BF16)
    core = place.core
    pieces = (
        (core * 1536, 1536 - core * 1536, core * 512),
        (512 + core * 512, 1024 - core * 512, 512 - core * 512),
    )

    def exchange(piece):
        theirs = pl.multiple_of(pieces[piece][1], 512)
        copies = []
        for p in range(PARTS):
            columns = pl.ds(WIDTH * p, WIDTH)
            copies.append(
                send(
                    gw_ref.at[pl.ds(theirs, 512), columns],
                    pair_ref.at[piece, :, columns],
                    pair_send.at[PARTS * piece + p],
                    pair_recv.at[PARTS * piece + p],
                    place.other_core(),
                )
            )
        return copies

    gw_ref[pl.ds(0, D), :] = tn(tok_ref[own_rows, :], gq_low).astype(BF16)
    att_low = att_ref[...].reshape(768, D).astype(BF16)
    gw_ref[pl.ds(3 * D, D), :] = tn(att_low, grad_ref[...]).astype(BF16)
    first_pair = exchange(0)
    gw_ref[pl.ds(D, D), :] = tn(tok_ref[...], gk_ref[...].astype(BF16)).astype(BF16)
    gw_ref[pl.ds(2 * D, D), :] = tn(tok_ref[...], gv_ref[...].astype(BF16)).astype(BF16)
    second_pair = exchange(1)
    u_ref[0:18] = to_tokens(pl.ds(0, 288)).reshape(18, 16, D)
    u_ref[18:36] = to_tokens(pl.ds(1056, 288)).reshape(18, 16, D)
    own = to_tokens(own_rows) + nt(gq_low, wq_ref[...])
    q_ref[...] = own.reshape(48, 16, D)

    for copy in along_lon:
        copy.wait_recv()

    def add_sides(ref, group, row, groups):
        for half in range(2):
            part = sides_ref[pl.ds(SIDE * half + row, 8 * groups), :].astype(F32)
            view = (pl.ds(group, groups), slice(8 * half, 8 * half + 8), slice(None))
            ref[view] = ref[view] + part.reshape(groups, 8, D)

    add_sides(u_ref, 0, 0, 18)
    add_sides(u_ref, 18, 528, 18)
    along_lat = []
    for i, dlat in enumerate((-1, 1)):
        strip = u_ref[pl.ds(18 * i, 18)].reshape(288, D).astype(BF16)
        k_ref[pl.ds(288 * i, 288), :] = strip
        copy = pltpu.make_async_remote_copy(
            src_ref=k_ref.at[pl.ds(288 * i, 288)],
            dst_ref=middle_ref.at[pl.ds(288 * i, 288)],
            send_sem=halo_send.at[2 + i],
            recv_sem=halo_recv.at[2 + i],
            device_id=place.near(dlat, 0),
            device_id_type=MESH,
        )
        guarded(place.inside[dlat], copy.start)
        along_lat.append((place.inside[dlat], place.inside[-dlat], copy))
    add_sides(q_ref, 0, 144, 48)

    mine = pl.multiple_of(core * 1024, 1024)
    acc_lanes = pl.ds(0, WIDTH)
    buffers = (recv0, recv1, recv2)
    staged = (0, 768, 960)
    pending = [[first_pair[p], second_pair[p]] for p in range(PARTS)]
    base = [0] * PARTS
    for stage in range(3):
        rows = BLOCKS[stage]
        incoming = buffers[stage]
        for p in range(PARTS):
            for copy in pending[p]:
                copy.wait_recv()
            if stage == 0:
                columns = pl.ds(WIDTH * p, WIDTH)
                for piece in range(2):
                    source, _, target = pieces[piece]
                    here = pl.ds(pl.multiple_of(source, 512), 512)
                    total = gw_ref[here, columns].astype(F32)
                    total = total + pair_ref[piece, :, columns].astype(F32)
                    s_ref[p, pl.ds(pl.multiple_of(target, 512), 512), acc_lanes] = total
            else:
                before = buffers[stage - 1]
                here = pl.ds(base[p], BLOCKS[stage - 1])
                total = s_ref[p, here, acc_lanes]
                for step in range(3):
                    total = total + before[p, step].astype(F32)
                s_ref[p, here, acc_lanes] = total
            axis = ORDERS[p][stage]
            me = place.index(axis)
            pending[p] = []
            for step in (1, 2, 3):
                block = base[p] + lax.rem(me + step, 4) * rows
                block = pl.multiple_of(block, rows)
                outgoing = p_ref.at[
                    p // 2,
                    pl.ds(staged[stage] + rows * (step - 1), rows),
                    pl.ds(WIDTH * (p % 2), WIDTH),
                ]
                outgoing[...] = s_ref[p, pl.ds(block, rows), acc_lanes].astype(BF16)
                slot = (p * 3 + stage) * 3 + step - 1
                pending[p].append(
                    send(
                        outgoing,
                        incoming.at[p, step - 1],
                        ring_send.at[slot],
                        ring_recv.at[slot],
                        place.along(axis, step),
                    )
                )
            base[p] = pl.multiple_of(base[p] + me * rows, rows)

    for stage in (3, 2, 1, 0):
        for p in range(PARTS):
            columns = pl.ds(WIDTH * p, WIDTH)
            for copy in pending[p]:
                copy.wait_recv()
            if stage == 3:
                total = s_ref[p, pl.ds(base[p], 16), acc_lanes]
                for step in range(3):
                    total = total + recv2[p, step].astype(F32)
                here = pl.ds(pl.multiple_of(mine + base[p], 16), 16)
                sum_ref[here, columns] = total.astype(BF16)
            if stage > 0:
                rows = BLOCKS[stage - 1]
                axis = ORDERS[p][stage - 1]
                here = pl.ds(pl.multiple_of(mine + base[p], rows), rows)
                here = sum_ref.at[here, columns]
                pending[p] = []
                for step in (1, 2, 3):
                    slot = (p * 3 + stage - 1) * 3 + step - 1
                    pending[p].append(
                        send(
                            here,
                            here,
                            back_send.at[slot],
                            back_recv.at[slot],
                            place.along(axis, step),
                        )
                    )
                base[p] = base[p] - place.index(axis) * rows
            else:
                here = sum_ref.at[pl.ds(mine, 1024), columns]
                pending[p] = [
                    send(here, here, last_send.at[p], last_recv.at[p], place.other_core())
                ]

    for sends, receives, copy in along_lat:
        guarded(sends, copy.wait_send)
        guarded(receives, copy.wait_recv)

    def edge(slot, first):
        rows = pl.ds(3 * first, 18)
        part = middle_ref[pl.ds(slot, 288), :].astype(F32).reshape(18, 16, D)
        q_ref[rows] = q_ref[rows] + part

    pl.when(place.lat < 7)(lambda: edge(0, 10))
    pl.when(place.lat > 0)(lambda: edge(288, 0))
    out_ref[...] = q_ref[...].reshape(768, D).astype(BF16)

    for p in range(PARTS):
        pending[p][0].wait_recv()
    for copy in waits:
        copy.wait_send()


def whole(x, g, w_query, w_key, w_value, w_out):
    dma = pltpu.SemaphoreType.DMA
    shapes = [
        ((ALL, D), BF16),
        ((768, D), BF16),
        ((4, D, D), BF16),
        ((ALL, D), BF16),
        ((ALL, D), BF16),
        ((D, 1536), BF16),
        ((D, 1536), BF16),
        ((48, 16, D), F32),
        ((48, 16, D), F32),
        ((ALL, D), F32),
        ((ALL, D), F32),
        ((48, 16, D), F32),
        ((48, 16, D), F32),
        ((6, 256, 256), BF16),
        ((6, 256, 256), BF16),
        ((6, 256, 256), BF16),
        ((2, KEYS, 384), F32),
        ((4, KEYS, 256), F32),
        ((2, KEYS, 256), BF16),
        ((KEYS, 256), BF16),
        ((4 * D, D), BF16),
        ((576, D), BF16),
        ((2 * SIDE, D), BF16),
        ((2, D, D), BF16),
    ]
    for rows in BLOCKS:
        shapes.append(((PARTS, 3, rows, WIDTH), BF16))
    scratch = [pltpu.VMEM(shape, kind) for shape, kind in shapes]
    scratch.append(dma((6,)))
    for count in (8, 4, 2 * PARTS, 9 * PARTS, 9 * PARTS, PARTS):
        scratch += [dma((count,))] * 2
    return pl.pallas_call(
        kernel,
        out_shape=(
            jax.ShapeDtypeStruct((768, D), BF16),
            jax.ShapeDtypeStruct((4 * D, D), BF16),
        ),
        in_specs=[pl.BlockSpec(memory_space=pl.ANY)] * 6,
        out_specs=(pl.BlockSpec(memory_space=pltpu.VMEM),) * 2,
        scratch_shapes=scratch,
        compiler_params=pltpu.CompilerParams(
            collective_id=0, has_side_effects=True, vmem_limit_bytes=62 * 1024 * 1024
        ),
    )(x, g, w_query, w_key, w_value, w_out)


def on_device(tokens, w_query, w_key, w_value, w_out, grad_out):
    x = tokens.transpose(0, 2, 1, 3).reshape(768, D)
    g = grad_out.transpose(0, 2, 1, 3).reshape(768, D)
    grad_tokens, sums = whole(x, g, w_query, w_key, w_value, w_out)
    grad_tokens = grad_tokens.reshape(16, 3, 16, D).transpose(0, 2, 1, 3)
    sums = sums.reshape(4, D, D).astype(F32)
    return grad_tokens, sums[0], sums[1], sums[2], sums[3]


def solution(mesh):
    placed = (P("lat", "lon", None, None), P(), P(), P(), P(), P("lat", "lon", None, None))
    return jax.shard_map(
        on_device,
        mesh=mesh,
        in_specs=placed,
        out_specs=(P("lat", "lon", None, None), P(), P(), P(), P()),
        check_vma=False,
    )
```

```python
import jax
import jax.numpy as jnp
from jax import lax
from jax.experimental import pallas as pl
from jax.experimental.pallas import tpu as pltpu
from jax.sharding import PartitionSpec as P

HEADS = 8
HEAD = 64
D = 512
RIM = 6
SPAN = 13
LATITUDES = 128
OWN = 28 * 48
SIDE = 28 * 24
ALL = OWN + 2 * SIDE
TQ = 96
KEYS = 768 + 384
CHUNK = 384
PARTS = 2
MESH = pl.DeviceIdType.MESH
F32 = jnp.float32
BF16 = jnp.bfloat16


def nn(a, b):
    return jnp.dot(a, b, preferred_element_type=F32)


def nt(a, b):
    return lax.dot_general(a, b, (((1,), (1,)), ((), ())), preferred_element_type=F32)


def tn(a, b):
    return lax.dot_general(a, b, (((0,), (0,)), ((), ())), preferred_element_type=F32)


AXES = (("x", "yz"), ("z", "yx"))
STEPS = [(i, j) for i in range(4) for j in range(4) if i or j]


class Place:
    def __init__(self):
        self.lat = lax.axis_index("lat")
        self.lon = lax.axis_index("lon")
        self.z = self.lat % 4
        self.core = self.lon % 2
        self.x = self.lon // 4
        self.y = (self.lat // 4) * 2 + (self.lon // 2) % 2
        self.inside = {-1: self.lat > 0, 0: None, 1: self.lat < 7}

    def near(self, dlat, dlon):
        return (self.lat + dlat, lax.rem(self.lon + dlon + 16, 16))

    def along(self, **steps):
        x = lax.rem(self.x + steps.get("x", 0), 4)
        y = lax.rem(self.y + steps.get("y", 0), 4)
        z = lax.rem(self.z + steps.get("z", 0), 4)
        return ((y // 2) * 4 + z, x * 4 + (y % 2) * 2 + self.core)

    def other_core(self):
        return (self.lat, self.lon + 1 - 2 * self.core)

    def index(self, axis):
        return {"x": self.x, "y": self.y, "z": self.z}[axis]


def guarded(condition, action):
    if condition is None:
        action()
    else:
        pl.when(condition)(action)


def halo_copies(place, send_sem, recv_sem, routes):
    copies = []
    for i, (dlat, dlon, source, target) in enumerate(routes):
        copy = pltpu.make_async_remote_copy(
            src_ref=source,
            dst_ref=target,
            send_sem=send_sem.at[i],
            recv_sem=recv_sem.at[i],
            device_id=place.near(dlat, dlon),
            device_id_type=MESH,
        )
        copies.append((dlat, place.inside[dlat], copy))
    return copies


def greet(place):
    barrier = pltpu.get_barrier_semaphore()
    for dlat in (-1, 0, 1):
        for dlon in (-1, 0, 1):
            if dlat or dlon:

                def signal(dlat=dlat, dlon=dlon):
                    pl.semaphore_signal(
                        barrier, inc=1, device_id=place.near(dlat, dlon), device_id_type=MESH
                    )

                guarded(place.inside[dlat], signal)
    rows = jnp.where(place.lat > 0, 3, 0) + jnp.where(place.lat < 7, 3, 0)
    return barrier, 2 + rows


def kernel(
    x_hbm,
    grad_hbm,
    wq_hbm,
    wk_hbm,
    wv_hbm,
    wo_hbm,
    out_ref,
    sum_ref,
    tok_ref,
    grad_ref,
    w_ref,
    k_ref,
    v_ref,
    kt_ref,
    vt_ref,
    q_ref,
    u_ref,
    gk_ref,
    gv_ref,
    gq_ref,
    att_ref,
    qbd_ref,
    ubd_ref,
    ubdt_ref,
    bias_ref,
    s_ref,
    p_ref,
    ds_ref,
    gw_ref,
    middle_ref,
    sides_ref,
    pair_ref,
    recv0,
    recv1,
    load_sem,
    gather_send,
    gather_recv,
    halo_send,
    halo_recv,
    pair_send,
    pair_recv,
    ring_send,
    ring_recv,
    plane_send,
    plane_recv,
    back_send,
    back_recv,
    ring_back_send,
    ring_back_recv,
    last_send,
    last_recv,
):
    place = Place()
    row0 = place.lat * 16
    wq_ref, wk_ref, wv_ref, wo_ref = [w_ref.at[i] for i in range(4)]
    own_rows = pl.ds(RIM * 48, 768)

    loads = [
        pltpu.make_async_copy(source, target, load_sem.at[i])
        for i, (source, target) in enumerate(
            (
                (x_hbm, tok_ref.at[own_rows]),
                (wk_hbm, wk_ref),
                (wv_hbm, wv_ref),
                (wq_hbm, wq_ref),
                (grad_hbm, grad_ref),
                (wo_hbm, wo_ref),
            )
        )
    ]
    for load in loads:
        load.start()

    barrier, count = greet(place)
    partners = [place.other_core()]
    partners += [place.along(y=i, z=j) for i, j in STEPS]
    partners += [place.along(y=i, x=j) for i, j in STEPS if j]
    for partner in partners:
        pl.semaphore_signal(barrier, inc=1, device_id=partner, device_id_type=MESH)

    loads[0].wait()
    x = tok_ref[own_rows, :].astype(F32).reshape(48, 16, D)
    gw_ref[0:384, :] = x[:, 0:8].reshape(384, D).astype(BF16)
    gw_ref[384:768, :] = x[:, 8:16].reshape(384, D).astype(BF16)
    pl.semaphore_wait(barrier, count + len(partners))

    strip_first = {-1: 22, 0: 6, 1: 0}
    lat_rows = {-1: (0, 6), 0: (0, 16), 1: (10, 6)}
    routes = []
    for dlat in (-1, 0, 1):
        begin, size = lat_rows[dlat]
        for dlon in (-1, 0, 1):
            first = strip_first[dlat]
            if dlon == 0:
                if dlat == 0:
                    continue
                source = tok_ref.at[pl.ds(48 * (RIM + begin), 48 * size)]
                target = tok_ref.at[pl.ds(48 * first, 48 * size)]
            else:
                half = 384 if dlon == 1 else 0
                side = OWN if dlon == 1 else OWN + SIDE
                source = gw_ref.at[pl.ds(half + 24 * begin, 24 * size)]
                target = tok_ref.at[pl.ds(side + 24 * first, 24 * size)]
            routes.append((dlat, dlon, source, target))
    gathered = halo_copies(place, gather_send, gather_recv, routes)
    for dlat, sends, copy in gathered:
        guarded(sends, copy.start)

    def clear(first):
        tok_ref[pl.ds(48 * first, 288), :] = jnp.zeros((288, D), BF16)
        tok_ref[pl.ds(OWN + 24 * first, 144), :] = jnp.zeros((144, D), BF16)
        tok_ref[pl.ds(OWN + SIDE + 24 * first, 144), :] = jnp.zeros((144, D), BF16)

    pl.when(place.lat == 0)(lambda: clear(0))
    pl.when(place.lat == 7)(lambda: clear(22))

    def project(rows):
        x = tok_ref[rows, :]
        k_ref[rows, :] = nn(x, wk_ref[...]).astype(BF16)
        v_ref[rows, :] = nn(x, wv_ref[...]).astype(BF16)

    loads[1].wait()
    loads[2].wait()
    project(own_rows)
    loads[3].wait()
    q = nn(tok_ref[own_rows, :], wq_ref[...]).astype(BF16).astype(F32) * 0.125
    q_ref[...] = q.reshape(48, 16, D)
    loads[4].wait()
    loads[5].wait()
    u = nt(grad_ref[...], wo_ref[...]).astype(BF16).astype(F32)
    u_ref[...] = u.reshape(48, 16, D)

    def zero(i, carry):
        rows = pl.ds(pl.multiple_of(i * 168, 168), 168)
        gk_ref[rows, :] = jnp.zeros((168, D), F32)
        gv_ref[rows, :] = jnp.zeros((168, D), F32)
        return carry

    lax.fori_loop(0, ALL // 168, zero, 0)

    head_row = lax.broadcasted_iota(jnp.int32, (256, 256), 0)
    feature = lax.broadcasted_iota(jnp.int32, (256, 256), 1)

    def diagonal(n):
        owner = (head_row + 256 * n) // TQ
        return owner == (feature + 128 * n) // HEAD

    def band_start(r):
        lowest = jnp.where(place.lat == 0, RIM, 0)
        highest = jnp.where(place.lat == 7, RIM, 12)
        return jnp.minimum(jnp.maximum(4 * r, lowest), highest)

    def fill_bias(r):
        base = band_start(r)
        lane = lax.broadcasted_iota(jnp.int32, (1, 384), 1) % TQ
        q_lat = row0 + 4 * r + lane // 24
        first = jnp.clip(q_lat - RIM, 0, LATITUDES - SPAN) - (row0 + base - RIM)
        q_col = lane % 8

        def bias(d_lat, d_col):
            inside = (d_lat >= 0) & (d_lat < SPAN) & (d_col >= 0) & (d_col < SPAN)
            return jnp.where(inside, 0.0, -jnp.inf)

        for c in range(2):
            key = lax.broadcasted_iota(jnp.int32, (768, 1), 0)
            rows = pl.ds(CHUNK * (1 - c), 768)
            bias_ref[c, rows, :] = bias(key // 48 - first, key % 16 - 8 * c - q_col + RIM)
            key = lax.broadcasted_iota(jnp.int32, (384, 1), 0)
            rows = pl.ds(768 * c, 384)
            bias_ref[c, rows, :] = bias(key // 24 - first, key % 8 + (16 * c - 8) - q_col + RIM)

    fill_bias(jnp.where(place.lat < 4, 0, 3))

    upward = place.lat < 4
    for dlat, _, copy in gathered:
        if dlat == 0:
            copy.wait_recv()
        elif dlat == 1:
            pl.when(upward & (place.lat > 0))(copy.wait_recv)
        else:
            pl.when((place.lat >= 4) & (place.lat < 7))(copy.wait_recv)
    project(pl.ds(pl.multiple_of(jnp.where(upward, 0, 1056), 96), 288))
    for side in (OWN, OWN + SIDE):
        project(pl.ds(pl.multiple_of(side + jnp.where(upward, 0, 144), 48), 528))

    def late_halo():
        for dlat, _, copy in gathered:
            if dlat == 1:
                pl.when(place.lat >= 4)(copy.wait_recv)
            elif dlat == -1:
                pl.when(upward)(copy.wait_recv)
        project(pl.ds(pl.multiple_of(jnp.where(upward, 1056, 0), 96), 288))
        for side in (OWN, OWN + SIDE):
            project(pl.ds(pl.multiple_of(side + jnp.where(upward, 528, 0), 48), 144))

    def latitude_band(i, carry):
        r = jnp.where(upward, i, 3 - i)
        base = band_start(r)
        pole = (place.lat == 0) | (place.lat == 7)
        pl.when(pole & ((i == 1) | (i == 2)))(lambda: fill_bias(r))
        pl.when(i == 2)(late_halo)
        own = [pl.multiple_of(base * 48 + 384 * i, 48) for i in range(2)]
        side = [pl.multiple_of(OWN + SIDE * c + base * 24, 48) for c in range(2)]
        for i, start in enumerate((side[0], own[0], own[1], side[1])):
            part = pl.ds(start, CHUNK)
            kt_ref[:, pl.ds(CHUNK * i, CHUNK)] = k_ref[part, :].T
            vt_ref[:, pl.ds(CHUNK * i, CHUNK)] = v_ref[part, :].T
        starts = ((side[0], own[0], own[1]), (own[0], own[1], side[1]))
        groups = pl.ds(12 * r, 12)

        for c in range(2):
            q_tile = q_ref[groups, 8 * c : 8 * c + 8, :].reshape(TQ, D).astype(BF16)
            u_tile = u_ref[groups, 8 * c : 8 * c + 8, :].reshape(TQ, D).astype(BF16)
            q_all = jnp.concatenate([q_tile] * HEADS, axis=0)
            u_all = jnp.concatenate([u_tile] * HEADS, axis=0)
            for n in range(3):
                keep = diagonal(n)
                block = q_all[256 * n : 256 * n + 256, 128 * n : 128 * n + 256]
                qbd_ref[3 * c + n] = jnp.where(keep, block, jnp.zeros_like(block))
                block = u_all[256 * n : 256 * n + 256, 128 * n : 128 * n + 256]
                block = jnp.where(keep, block, jnp.zeros_like(block))
                ubd_ref[3 * c + n] = block
                ubdt_ref[3 * c + n] = block.T
            att_ref[groups, 8 * c : 8 * c + 8, :] = jnp.zeros((12, 8, D), F32)
            gq_ref[groups, 8 * c : 8 * c + 8, :] = jnp.zeros((12, 8, D), F32)

        def fold(ref, c, n, block):
            block = jnp.where(diagonal(n), block, 0.0)
            row = 256 * n
            while row < 256 * n + 256:
                h = row // TQ
                end = min(TQ * (h + 1), 256 * n + 256)
                begin = row - TQ * h
                count = (end - row) // 8
                view = (
                    pl.ds(12 * r + begin // 8, count),
                    slice(8 * c, 8 * c + 8),
                    slice(128 * n, 128 * n + 256),
                )
                ref[view] += block[row - 256 * n : end - 256 * n].reshape(count, 8, 256)
                row = end

        state = [{} for _ in range(6)]

        def parts(b):
            return b // 3, b % 3, pl.ds(128 * (b % 3), 256)

        def score(b):
            c, n, feats = parts(b)
            bias_lanes = ((0, 128), (256, 0), (128, 256))[n]
            high = jnp.full((8, 256), -jnp.inf, F32)
            for j in range(3):
                part = pl.ds(CHUNK * j, CHUNK)
                x = nt(k_ref[pl.ds(starts[c][j], CHUNK), feats], qbd_ref[b])
                x = x + jnp.concatenate(
                    [bias_ref[c, part, pl.ds(lane, 128)] for lane in bias_lanes], axis=1
                )
                s_ref[b % 4, part, :] = x
                high = jnp.maximum(high, jnp.max(x.reshape(CHUNK // 8, 8, 256), axis=0))
                yield
            state[b]["high"] = jnp.max(high, axis=0, keepdims=True)

        def exponent(b):
            high = state[b]["high"]
            total = jnp.zeros((8, 256), F32)
            for j in range(3):
                part = pl.ds(CHUNK * j, CHUNK)
                e = jnp.exp(s_ref[b % 4, part, :] - high)
                s_ref[b % 4, part, :] = e
                total = total + jnp.sum(e.reshape(CHUNK // 8, 8, 256), axis=0)
                yield
            state[b]["scale"] = 1.0 / jnp.sum(total, axis=0, keepdims=True)

        def attend(b):
            c, n, feats = parts(b)
            scale = state[b]["scale"]
            for j in range(3):
                part = pl.ds(CHUNK * j, CHUNK)
                p = s_ref[b % 4, part, :] * scale
                s_ref[b % 4, part, :] = p
                p_ref[b % 2, part, :] = p.astype(BF16)
                yield
            out_t = nn(vt_ref[feats, pl.ds(CHUNK * c, KEYS)], p_ref[b % 2])
            out_t = out_t.astype(BF16).astype(F32)
            state[b]["row_dot"] = jnp.sum(out_t * ubdt_ref[b].astype(F32), axis=0, keepdims=True)
            fold(att_ref, c, n, out_t.T)

        def gradient(b):
            c, n, feats = parts(b)
            row_dot = state[b]["row_dot"]
            for j in range(3):
                part = pl.ds(CHUNK * j, CHUNK)
                rows = pl.ds(starts[c][j], CHUNK)
                grad_p = nt(v_ref[rows, feats], ubd_ref[b])
                ds = (s_ref[b % 4, part, :] * (grad_p - row_dot)).astype(BF16)
                ds_ref[part, :] = ds
                gv_ref[rows, feats] += nn(p_ref[b % 2, part, :], ubd_ref[b])
                gk_ref[rows, feats] += nn(ds, qbd_ref[b])
                yield
            gq_t = nn(kt_ref[feats, pl.ds(CHUNK * c, KEYS)], ds_ref[...])
            fold(gq_ref, c, n, gq_t.T)

        stages = (score, exponent, attend, gradient)
        for step in range(6 + len(stages) - 1):
            running = [
                stage(step - i) for i, stage in enumerate(stages) if 0 <= step - i < 6
            ]
            while running:
                running = [g for g in running if next(g, running) is None]
        return carry

    lax.fori_loop(0, 4, latitude_band, 0)

    def send(source, target, send_sem, recv_sem, device):
        copy = pltpu.make_async_remote_copy(
            src_ref=source,
            dst_ref=target,
            send_sem=send_sem,
            recv_sem=recv_sem,
            device_id=device,
            device_id_type=MESH,
        )
        copy.start()
        waits.append(copy)
        return copy

    waits = []

    def to_tokens(rows):
        gk_low = gk_ref[rows, :].astype(BF16)
        gv_low = gv_ref[rows, :].astype(BF16)
        return nt(gk_low, wk_ref[...]) + nt(gv_low, wv_ref[...])

    for dlat, sends, copy in gathered:
        guarded(sends, copy.wait_send)
    along_lon = []
    for i, (dlon, source, target) in enumerate(((-1, OWN, SIDE), (1, OWN + SIDE, 0))):
        k_ref[pl.ds(source, SIDE), :] = to_tokens(pl.ds(source, SIDE)).astype(BF16)
        along_lon.append(
            send(
                k_ref.at[pl.ds(source, SIDE)],
                sides_ref.at[pl.ds(target, SIDE)],
                halo_send.at[i],
                halo_recv.at[i],
                place.near(0, dlon),
            )
        )

    gq_low = (gq_ref[...].reshape(768, D) * 0.125).astype(BF16)
    core = place.core
    pieces = (
        (core * 1536, 1536 - core * 1536),
        (512 + core * 512, 1024 - core * 512),
    )

    first_rows = [pl.multiple_of(piece[0], 512) for piece in pieces]
    pending = [None] * PARTS
    quarter = [pl.multiple_of(place.index(AXES[p][0]) * 128, 128) for p in range(PARTS)]
    slot_rows = []
    slot_lanes = []
    for p in range(PARTS):
        one, two = AXES[p][1]
        index = place.index(one) * 4 + place.index(two)
        slot_rows.append(pl.multiple_of(index // 2 * 16, 16))
        slot_lanes.append(pl.multiple_of(index % 2 * 256, 256))
    totals = (gq_ref, att_ref)

    def exchange(p):
        theirs = pl.multiple_of(pieces[p][1], 512)
        source = gw_ref.at[pl.ds(theirs, 512)]
        pending[p] = [
            send(source, pair_ref.at[p], pair_send.at[p], pair_recv.at[p], place.other_core())
        ]

    def arrive(p):
        for copy in pending[p]:
            copy.wait_recv()
        pending[p] = []

    def ring(p):
        arrive(p)
        total = gw_ref[pl.ds(first_rows[p], 512), :].astype(F32) + pair_ref[p].astype(F32)
        totals[p][0:32] = total.reshape(32, 16, D)
        axis = AXES[p][0]
        me = place.index(axis)
        for step in (1, 2, 3):
            block = lax.rem(me + step, 4) * 8
            outgoing = v_ref.at[pl.ds(1024 * p + 128 * (step - 1), 128)]
            outgoing[...] = totals[p][pl.ds(block, 8)].reshape(128, D).astype(BF16)
            slot = p * 3 + step - 1
            pending[p].append(
                send(
                    outgoing,
                    recv0.at[p, step - 1],
                    ring_send.at[slot],
                    ring_recv.at[slot],
                    place.along(**{axis: step}),
                )
            )

    def plane(p):
        arrive(p)
        axis = AXES[p][0]
        here = pl.ds(place.index(axis) * 8, 8)
        total = totals[p][here].reshape(128, D)
        for step in range(3):
            total = total + recv0[p, step].astype(F32)
        totals[p][here] = total.reshape(8, 16, D)
        first = 1024 * p + 384
        v_ref[pl.ds(first, 128), :] = total.astype(BF16)
        one, two = AXES[p][1]
        a, b = place.index(one), place.index(two)
        for k, (i, j) in enumerate(STEPS):
            block = lax.rem(a + i, 4) * 4 + lax.rem(b + j, 4)
            row = pl.multiple_of(first + block // 2 * 16, 16)
            lane = pl.multiple_of(block % 2 * 256, 256)
            slot = p * 15 + k
            pending[p].append(
                send(
                    v_ref.at[pl.ds(row, 16), pl.ds(lane, 256)],
                    recv1.at[p, k],
                    plane_send.at[slot],
                    plane_recv.at[slot],
                    place.along(**{one: i, two: j}),
                )
            )

    def plane_back(p):
        arrive(p)
        lanes = pl.ds(slot_lanes[p], 256)
        group = place.index(AXES[p][0]) * 8 + slot_rows[p] // 16
        total = totals[p][group, :, lanes]
        for k in range(15):
            total = total + recv1[p, k].astype(F32)
        row = pl.multiple_of(first_rows[p] + quarter[p] + slot_rows[p], 16)
        sum_ref[pl.ds(row, 16), lanes] = total.astype(BF16)
        here = sum_ref.at[pl.ds(row, 16), lanes]
        one, two = AXES[p][1]
        for k, (i, j) in enumerate(STEPS):
            slot = p * 15 + k
            pending[p].append(
                send(
                    here,
                    here,
                    back_send.at[slot],
                    back_recv.at[slot],
                    place.along(**{one: i, two: j}),
                )
            )

    def ring_back(p):
        arrive(p)
        here = sum_ref.at[pl.ds(pl.multiple_of(first_rows[p] + quarter[p], 128), 128)]
        for step in (1, 2, 3):
            slot = p * 3 + step - 1
            pending[p].append(
                send(
                    here,
                    here,
                    ring_back_send.at[slot],
                    ring_back_recv.at[slot],
                    place.along(**{AXES[p][0]: step}),
                )
            )

    def pair_back(p):
        arrive(p)
        here = sum_ref.at[pl.ds(first_rows[p], 512)]
        pending[p] = [send(here, here, last_send.at[p], last_recv.at[p], place.other_core())]

    gw_ref[pl.ds(0, D), :] = tn(tok_ref[own_rows, :], gq_low).astype(BF16)
    att_low = att_ref[...].reshape(768, D).astype(BF16)
    gw_ref[pl.ds(3 * D, D), :] = tn(att_low, grad_ref[...]).astype(BF16)
    exchange(0)
    gw_ref[pl.ds(D, D), :] = tn(tok_ref[...], gk_ref[...].astype(BF16)).astype(BF16)
    gw_ref[pl.ds(2 * D, D), :] = tn(tok_ref[...], gv_ref[...].astype(BF16)).astype(BF16)
    exchange(1)
    ring(0)
    u_ref[0:18] = to_tokens(pl.ds(0, 288)).reshape(18, 16, D)
    u_ref[18:36] = to_tokens(pl.ds(1056, 288)).reshape(18, 16, D)
    own = to_tokens(own_rows) + nt(gq_low, wq_ref[...])
    q_ref[...] = own.reshape(48, 16, D)
    ring(1)
    plane(0)

    for copy in along_lon:
        copy.wait_recv()

    def add_sides(ref, group, row, groups):
        for half in range(2):
            part = sides_ref[pl.ds(SIDE * half + row, 8 * groups), :].astype(F32)
            view = (pl.ds(group, groups), slice(8 * half, 8 * half + 8), slice(None))
            ref[view] = ref[view] + part.reshape(groups, 8, D)

    add_sides(u_ref, 0, 0, 18)
    add_sides(u_ref, 18, 528, 18)
    along_lat = []
    for i, dlat in enumerate((-1, 1)):
        strip = u_ref[pl.ds(18 * i, 18)].reshape(288, D).astype(BF16)
        k_ref[pl.ds(288 * i, 288), :] = strip
        copy = pltpu.make_async_remote_copy(
            src_ref=k_ref.at[pl.ds(288 * i, 288)],
            dst_ref=middle_ref.at[pl.ds(288 * i, 288)],
            send_sem=halo_send.at[2 + i],
            recv_sem=halo_recv.at[2 + i],
            device_id=place.near(dlat, 0),
            device_id_type=MESH,
        )
        guarded(place.inside[dlat], copy.start)
        along_lat.append((place.inside[dlat], place.inside[-dlat], copy))
    add_sides(q_ref, 0, 144, 48)

    plane_back(0)
    plane(1)
    ring_back(0)
    plane_back(1)
    pair_back(0)
    ring_back(1)
    pair_back(1)

    for sends, receives, copy in along_lat:
        guarded(sends, copy.wait_send)
        guarded(receives, copy.wait_recv)

    def edge(slot, first):
        rows = pl.ds(3 * first, 18)
        part = middle_ref[pl.ds(slot, 288), :].astype(F32).reshape(18, 16, D)
        q_ref[rows] = q_ref[rows] + part

    pl.when(place.lat < 7)(lambda: edge(0, 10))
    pl.when(place.lat > 0)(lambda: edge(288, 0))
    out_ref[...] = q_ref[...].reshape(768, D).astype(BF16)

    for p in range(PARTS):
        pending[p][0].wait_recv()
    for copy in waits:
        copy.wait_send()


def whole(x, g, w_query, w_key, w_value, w_out):
    dma = pltpu.SemaphoreType.DMA
    shapes = [
        ((ALL, D), BF16),
        ((768, D), BF16),
        ((4, D, D), BF16),
        ((ALL, D), BF16),
        ((ALL, D), BF16),
        ((D, 1536), BF16),
        ((D, 1536), BF16),
        ((48, 16, D), F32),
        ((48, 16, D), F32),
        ((ALL, D), F32),
        ((ALL, D), F32),
        ((48, 16, D), F32),
        ((48, 16, D), F32),
        ((6, 256, 256), BF16),
        ((6, 256, 256), BF16),
        ((6, 256, 256), BF16),
        ((2, KEYS, 384), F32),
        ((4, KEYS, 256), F32),
        ((2, KEYS, 256), BF16),
        ((KEYS, 256), BF16),
        ((4 * D, D), BF16),
        ((576, D), BF16),
        ((2 * SIDE, D), BF16),
        ((2, D, D), BF16),
    ]
    shapes += [((PARTS, 3, 128, D), BF16), ((PARTS, 15, 16, 256), BF16)]
    scratch = [pltpu.VMEM(shape, kind) for shape, kind in shapes]
    scratch.append(dma((6,)))
    for count in (8, 4, PARTS, 3 * PARTS, 15 * PARTS, 15 * PARTS, 3 * PARTS, PARTS):
        scratch += [dma((count,))] * 2
    return pl.pallas_call(
        kernel,
        out_shape=(
            jax.ShapeDtypeStruct((768, D), BF16),
            jax.ShapeDtypeStruct((4 * D, D), BF16),
        ),
        in_specs=[pl.BlockSpec(memory_space=pl.ANY)] * 6,
        out_specs=(pl.BlockSpec(memory_space=pltpu.VMEM),) * 2,
        scratch_shapes=scratch,
        compiler_params=pltpu.CompilerParams(
            collective_id=0, has_side_effects=True, vmem_limit_bytes=62 * 1024 * 1024
        ),
    )(x, g, w_query, w_key, w_value, w_out)


def on_device(tokens, w_query, w_key, w_value, w_out, grad_out):
    x = tokens.transpose(0, 2, 1, 3).reshape(768, D)
    g = grad_out.transpose(0, 2, 1, 3).reshape(768, D)
    grad_tokens, sums = whole(x, g, w_query, w_key, w_value, w_out)
    grad_tokens = grad_tokens.reshape(16, 3, 16, D).transpose(0, 2, 1, 3)
    sums = sums.reshape(4, D, D).astype(F32)
    return grad_tokens, sums[0], sums[1], sums[2], sums[3]


def solution(mesh):
    placed = (P("lat", "lon", None, None), P(), P(), P(), P(), P("lat", "lon", None, None))
    return jax.shard_map(
        on_device,
        mesh=mesh,
        in_specs=placed,
        out_specs=(P("lat", "lon", None, None), P(), P(), P(), P()),
        check_vma=False,
    )
```

```python
import jax
import jax.numpy as jnp
from jax import lax
from jax.experimental import pallas as pl
from jax.experimental.pallas import tpu as pltpu
from jax.sharding import PartitionSpec as P

HEADS = 8
HEAD = 64
D = 512
RIM = 6
SPAN = 13
LATITUDES = 128
OWN = 28 * 48
SIDE = 28 * 24
ALL = OWN + 2 * SIDE
TQ = 96
KEYS = 768 + 384
CHUNK = 384
PARTS = 2
MESH = pl.DeviceIdType.MESH
F32 = jnp.float32
BF16 = jnp.bfloat16


def nn(a, b):
    return jnp.dot(a, b, preferred_element_type=F32)


def nt(a, b):
    return lax.dot_general(a, b, (((1,), (1,)), ((), ())), preferred_element_type=F32)


def tn(a, b):
    return lax.dot_general(a, b, (((0,), (0,)), ((), ())), preferred_element_type=F32)


AXES = (("x", "yz"), ("z", "yx"))
STEPS = [(i, j) for i in range(4) for j in range(4) if i or j]


class Place:
    def __init__(self):
        self.lat = lax.axis_index("lat")
        self.lon = lax.axis_index("lon")
        self.z = self.lat % 4
        self.core = self.lon % 2
        self.x = self.lon // 4
        self.y = (self.lat // 4) * 2 + (self.lon // 2) % 2
        self.inside = {-1: self.lat > 0, 0: None, 1: self.lat < 7}

    def near(self, dlat, dlon):
        return (self.lat + dlat, lax.rem(self.lon + dlon + 16, 16))

    def along(self, **steps):
        x = lax.rem(self.x + steps.get("x", 0), 4)
        y = lax.rem(self.y + steps.get("y", 0), 4)
        z = lax.rem(self.z + steps.get("z", 0), 4)
        return ((y // 2) * 4 + z, x * 4 + (y % 2) * 2 + self.core)

    def other_core(self):
        return (self.lat, self.lon + 1 - 2 * self.core)

    def index(self, axis):
        return {"x": self.x, "y": self.y, "z": self.z}[axis]


def guarded(condition, action):
    if condition is None:
        action()
    else:
        pl.when(condition)(action)


def halo_copies(place, send_sem, recv_sem, routes):
    copies = []
    for i, (dlat, dlon, source, target) in enumerate(routes):
        copy = pltpu.make_async_remote_copy(
            src_ref=source,
            dst_ref=target,
            send_sem=send_sem.at[i],
            recv_sem=recv_sem.at[i],
            device_id=place.near(dlat, dlon),
            device_id_type=MESH,
        )
        copies.append((dlat, place.inside[dlat], copy))
    return copies


def greet(place):
    barrier = pltpu.get_barrier_semaphore()
    for dlat in (-1, 0, 1):
        for dlon in (-1, 0, 1):
            if dlat or dlon:

                def signal(dlat=dlat, dlon=dlon):
                    pl.semaphore_signal(
                        barrier, inc=1, device_id=place.near(dlat, dlon), device_id_type=MESH
                    )

                guarded(place.inside[dlat], signal)
    rows = jnp.where(place.lat > 0, 3, 0) + jnp.where(place.lat < 7, 3, 0)
    return barrier, 2 + rows


def kernel(
    x_hbm,
    grad_hbm,
    wq_hbm,
    wk_hbm,
    wv_hbm,
    wo_hbm,
    out_ref,
    sum_ref,
    tok_ref,
    grad_ref,
    w_ref,
    k_ref,
    v_ref,
    kt_ref,
    vt_ref,
    q_ref,
    u_ref,
    gk_ref,
    gv_ref,
    gq_ref,
    att_ref,
    qbd_ref,
    ubd_ref,
    ubdt_ref,
    bias_ref,
    s_ref,
    p_ref,
    ds_ref,
    gw_ref,
    middle_ref,
    sides_ref,
    pair_ref,
    recv0,
    recv1,
    load_sem,
    gather_send,
    gather_recv,
    halo_send,
    halo_recv,
    pair_send,
    pair_recv,
    ring_send,
    ring_recv,
    plane_send,
    plane_recv,
    back_send,
    back_recv,
    ring_back_send,
    ring_back_recv,
    last_send,
    last_recv,
):
    place = Place()
    row0 = place.lat * 16
    wq_ref, wk_ref, wv_ref, wo_ref = [w_ref.at[i] for i in range(4)]
    own_rows = pl.ds(RIM * 48, 768)

    loads = [
        pltpu.make_async_copy(source, target, load_sem.at[i])
        for i, (source, target) in enumerate(
            (
                (x_hbm, tok_ref.at[own_rows]),
                (wk_hbm, wk_ref),
                (wv_hbm, wv_ref),
                (wq_hbm, wq_ref),
                (grad_hbm, grad_ref),
                (wo_hbm, wo_ref),
            )
        )
    ]
    for load in loads:
        load.start()

    barrier, count = greet(place)
    partners = [place.other_core()]
    partners += [place.along(y=i, z=j) for i, j in STEPS]
    partners += [place.along(y=i, x=j) for i, j in STEPS if j]
    for partner in partners:
        pl.semaphore_signal(barrier, inc=1, device_id=partner, device_id_type=MESH)

    loads[0].wait()
    x = tok_ref[own_rows, :].astype(F32).reshape(48, 16, D)
    gw_ref[0:384, :] = x[:, 0:8].reshape(384, D).astype(BF16)
    gw_ref[384:768, :] = x[:, 8:16].reshape(384, D).astype(BF16)
    pl.semaphore_wait(barrier, count + len(partners))

    strip_first = {-1: 22, 0: 6, 1: 0}
    lat_rows = {-1: (0, 6), 0: (0, 16), 1: (10, 6)}
    routes = []
    for dlat in (-1, 0, 1):
        begin, size = lat_rows[dlat]
        for dlon in (-1, 0, 1):
            first = strip_first[dlat]
            if dlon == 0:
                if dlat == 0:
                    continue
                source = tok_ref.at[pl.ds(48 * (RIM + begin), 48 * size)]
                target = tok_ref.at[pl.ds(48 * first, 48 * size)]
            else:
                half = 384 if dlon == 1 else 0
                side = OWN if dlon == 1 else OWN + SIDE
                source = gw_ref.at[pl.ds(half + 24 * begin, 24 * size)]
                target = tok_ref.at[pl.ds(side + 24 * first, 24 * size)]
            routes.append((dlat, dlon, source, target))
    gathered = halo_copies(place, gather_send, gather_recv, routes)
    for dlat, sends, copy in gathered:
        guarded(sends, copy.start)

    def clear(first):
        tok_ref[pl.ds(48 * first, 288), :] = jnp.zeros((288, D), BF16)
        tok_ref[pl.ds(OWN + 24 * first, 144), :] = jnp.zeros((144, D), BF16)
        tok_ref[pl.ds(OWN + SIDE + 24 * first, 144), :] = jnp.zeros((144, D), BF16)

    pl.when(place.lat == 0)(lambda: clear(0))
    pl.when(place.lat == 7)(lambda: clear(22))

    def project(rows):
        x = tok_ref[rows, :]
        k_ref[rows, :] = nn(x, wk_ref[...]).astype(BF16)
        v_ref[rows, :] = nn(x, wv_ref[...]).astype(BF16)

    loads[1].wait()
    loads[2].wait()
    project(own_rows)
    loads[3].wait()
    q = nn(tok_ref[own_rows, :], wq_ref[...]).astype(BF16).astype(F32) * 0.125
    q_ref[...] = q.reshape(48, 16, D)
    loads[4].wait()
    loads[5].wait()
    u = nt(grad_ref[...], wo_ref[...]).astype(BF16).astype(F32)
    u_ref[...] = u.reshape(48, 16, D)

    def zero(i, carry):
        rows = pl.ds(pl.multiple_of(i * 168, 168), 168)
        gk_ref[rows, :] = jnp.zeros((168, D), F32)
        gv_ref[rows, :] = jnp.zeros((168, D), F32)
        return carry

    lax.fori_loop(0, ALL // 168, zero, 0)

    head_row = lax.broadcasted_iota(jnp.int32, (256, 256), 0)
    feature = lax.broadcasted_iota(jnp.int32, (256, 256), 1)

    def diagonal(n):
        owner = (head_row + 256 * n) // TQ
        return owner == (feature + 128 * n) // HEAD

    def band_start(r):
        lowest = jnp.where(place.lat == 0, RIM, 0)
        highest = jnp.where(place.lat == 7, RIM, 12)
        return jnp.minimum(jnp.maximum(4 * r, lowest), highest)

    def fill_bias(r):
        base = band_start(r)
        lane = lax.broadcasted_iota(jnp.int32, (1, 384), 1) % TQ
        q_lat = row0 + 4 * r + lane // 24
        first = jnp.clip(q_lat - RIM, 0, LATITUDES - SPAN) - (row0 + base - RIM)
        q_col = lane % 8

        def bias(d_lat, d_col):
            inside = (d_lat >= 0) & (d_lat < SPAN) & (d_col >= 0) & (d_col < SPAN)
            return jnp.where(inside, 0.0, -jnp.inf)

        for c in range(2):
            key = lax.broadcasted_iota(jnp.int32, (768, 1), 0)
            rows = pl.ds(CHUNK * (1 - c), 768)
            bias_ref[c, rows, :] = bias(key // 48 - first, key % 16 - 8 * c - q_col + RIM)
            key = lax.broadcasted_iota(jnp.int32, (384, 1), 0)
            rows = pl.ds(768 * c, 384)
            bias_ref[c, rows, :] = bias(key // 24 - first, key % 8 + (16 * c - 8) - q_col + RIM)

    fill_bias(jnp.where(place.lat < 4, 0, 3))

    upward = place.lat < 4
    for dlat, _, copy in gathered:
        if dlat == 0:
            copy.wait_recv()
        elif dlat == 1:
            pl.when(upward & (place.lat > 0))(copy.wait_recv)
        else:
            pl.when((place.lat >= 4) & (place.lat < 7))(copy.wait_recv)
    project(pl.ds(pl.multiple_of(jnp.where(upward, 0, 1056), 96), 288))
    for side in (OWN, OWN + SIDE):
        project(pl.ds(pl.multiple_of(side + jnp.where(upward, 0, 144), 48), 528))

    def late_halo():
        for dlat, _, copy in gathered:
            if dlat == 1:
                pl.when(place.lat >= 4)(copy.wait_recv)
            elif dlat == -1:
                pl.when(upward)(copy.wait_recv)
        project(pl.ds(pl.multiple_of(jnp.where(upward, 1056, 0), 96), 288))
        for side in (OWN, OWN + SIDE):
            project(pl.ds(pl.multiple_of(side + jnp.where(upward, 528, 0), 48), 144))

    def latitude_band(i, carry):
        r = jnp.where(upward, i, 3 - i)
        base = band_start(r)
        pole = (place.lat == 0) | (place.lat == 7)
        pl.when(pole & ((i == 1) | (i == 2)))(lambda: fill_bias(r))
        pl.when(i == 2)(late_halo)
        own = [pl.multiple_of(base * 48 + 384 * i, 48) for i in range(2)]
        side = [pl.multiple_of(OWN + SIDE * c + base * 24, 48) for c in range(2)]
        for i, start in enumerate((side[0], own[0], own[1], side[1])):
            part = pl.ds(start, CHUNK)
            kt_ref[:, pl.ds(CHUNK * i, CHUNK)] = k_ref[part, :].T
            vt_ref[:, pl.ds(CHUNK * i, CHUNK)] = v_ref[part, :].T
        starts = ((side[0], own[0], own[1]), (own[0], own[1], side[1]))
        groups = pl.ds(12 * r, 12)

        for c in range(2):
            q_tile = q_ref[groups, 8 * c : 8 * c + 8, :].reshape(TQ, D).astype(BF16)
            u_tile = u_ref[groups, 8 * c : 8 * c + 8, :].reshape(TQ, D).astype(BF16)
            q_all = jnp.concatenate([q_tile] * HEADS, axis=0)
            u_all = jnp.concatenate([u_tile] * HEADS, axis=0)
            for n in range(3):
                keep = diagonal(n)
                block = q_all[256 * n : 256 * n + 256, 128 * n : 128 * n + 256]
                qbd_ref[3 * c + n] = jnp.where(keep, block, jnp.zeros_like(block))
                block = u_all[256 * n : 256 * n + 256, 128 * n : 128 * n + 256]
                block = jnp.where(keep, block, jnp.zeros_like(block))
                ubd_ref[3 * c + n] = block
                ubdt_ref[3 * c + n] = block.T
            att_ref[groups, 8 * c : 8 * c + 8, :] = jnp.zeros((12, 8, D), F32)
            gq_ref[groups, 8 * c : 8 * c + 8, :] = jnp.zeros((12, 8, D), F32)

        def fold(ref, c, n, block):
            block = jnp.where(diagonal(n), block, 0.0)
            row = 256 * n
            while row < 256 * n + 256:
                h = row // TQ
                end = min(TQ * (h + 1), 256 * n + 256)
                begin = row - TQ * h
                count = (end - row) // 8
                view = (
                    pl.ds(12 * r + begin // 8, count),
                    slice(8 * c, 8 * c + 8),
                    slice(128 * n, 128 * n + 256),
                )
                ref[view] += block[row - 256 * n : end - 256 * n].reshape(count, 8, 256)
                row = end

        state = [{} for _ in range(6)]

        def parts(b):
            return b // 3, b % 3, pl.ds(128 * (b % 3), 256)

        def score(b):
            c, n, feats = parts(b)
            bias_lanes = ((0, 128), (256, 0), (128, 256))[n]
            high = jnp.full((8, 256), -jnp.inf, F32)
            for j in range(3):
                part = pl.ds(CHUNK * j, CHUNK)
                x = nt(k_ref[pl.ds(starts[c][j], CHUNK), feats], qbd_ref[b])
                x = x + jnp.concatenate(
                    [bias_ref[c, part, pl.ds(lane, 128)] for lane in bias_lanes], axis=1
                )
                s_ref[b % 4, part, :] = x
                high = jnp.maximum(high, jnp.max(x.reshape(CHUNK // 8, 8, 256), axis=0))
                yield
            state[b]["high"] = jnp.max(high, axis=0, keepdims=True)

        def exponent(b):
            high = state[b]["high"]
            total = jnp.zeros((8, 256), F32)
            for j in range(3):
                part = pl.ds(CHUNK * j, CHUNK)
                e = jnp.exp(s_ref[b % 4, part, :] - high)
                s_ref[b % 4, part, :] = e
                total = total + jnp.sum(e.reshape(CHUNK // 8, 8, 256), axis=0)
                yield
            state[b]["scale"] = 1.0 / jnp.sum(total, axis=0, keepdims=True)

        def attend(b):
            c, n, feats = parts(b)
            scale = state[b]["scale"]
            for j in range(3):
                part = pl.ds(CHUNK * j, CHUNK)
                p_ref[b % 2, part, :] = (s_ref[b % 4, part, :] * scale).astype(BF16)
                yield
            out_t = nn(vt_ref[feats, pl.ds(CHUNK * c, KEYS)], p_ref[b % 2])
            out_t = out_t.astype(BF16).astype(F32)
            state[b]["row_dot"] = jnp.sum(out_t * ubdt_ref[b].astype(F32), axis=0, keepdims=True)
            fold(att_ref, c, n, out_t.T)

        def gradient(b):
            c, n, feats = parts(b)
            row_dot = state[b]["row_dot"]
            scale = state[b]["scale"]
            for j in range(3):
                part = pl.ds(CHUNK * j, CHUNK)
                rows = pl.ds(starts[c][j], CHUNK)
                grad_p = nn(v_ref[rows, feats], ubdt_ref[b])
                ds = (s_ref[b % 4, part, :] * scale * (grad_p - row_dot)).astype(BF16)
                ds_ref[part, :] = ds
                gv_ref[rows, feats] += nn(p_ref[b % 2, part, :], ubd_ref[b])
                gk_ref[rows, feats] += nn(ds, qbd_ref[b])
                yield
            gq_t = nn(kt_ref[feats, pl.ds(CHUNK * c, KEYS)], ds_ref[...])
            fold(gq_ref, c, n, gq_t.T)

        stages = (score, exponent, attend, gradient)
        for step in range(6 + len(stages) - 1):
            running = [
                stage(step - i) for i, stage in enumerate(stages) if 0 <= step - i < 6
            ]
            while running:
                running = [g for g in running if next(g, running) is None]
        return carry

    lax.fori_loop(0, 4, latitude_band, 0)

    def send(source, target, send_sem, recv_sem, device):
        copy = pltpu.make_async_remote_copy(
            src_ref=source,
            dst_ref=target,
            send_sem=send_sem,
            recv_sem=recv_sem,
            device_id=device,
            device_id_type=MESH,
        )
        copy.start()
        waits.append(copy)
        return copy

    waits = []

    def to_tokens(rows):
        gk_low = gk_ref[rows, :].astype(BF16)
        gv_low = gv_ref[rows, :].astype(BF16)
        return nt(gk_low, wk_ref[...]) + nt(gv_low, wv_ref[...])

    for dlat, sends, copy in gathered:
        guarded(sends, copy.wait_send)
    along_lon = []
    for i, (dlon, source, target) in enumerate(((-1, OWN, SIDE), (1, OWN + SIDE, 0))):
        k_ref[pl.ds(source, SIDE), :] = to_tokens(pl.ds(source, SIDE)).astype(BF16)
        along_lon.append(
            send(
                k_ref.at[pl.ds(source, SIDE)],
                sides_ref.at[pl.ds(target, SIDE)],
                halo_send.at[i],
                halo_recv.at[i],
                place.near(0, dlon),
            )
        )

    gq_low = (gq_ref[...].reshape(768, D) * 0.125).astype(BF16)
    core = place.core
    pieces = (
        (core * 1536, 1536 - core * 1536),
        (512 + core * 512, 1024 - core * 512),
    )

    first_rows = [pl.multiple_of(piece[0], 512) for piece in pieces]
    pending = [None] * PARTS
    quarter = [pl.multiple_of(place.index(AXES[p][0]) * 128, 128) for p in range(PARTS)]
    slot_rows = []
    slot_lanes = []
    for p in range(PARTS):
        one, two = AXES[p][1]
        index = place.index(one) * 4 + place.index(two)
        slot_rows.append(pl.multiple_of(index // 2 * 16, 16))
        slot_lanes.append(pl.multiple_of(index % 2 * 256, 256))
    totals = (gq_ref, att_ref)

    def exchange(p):
        theirs = pl.multiple_of(pieces[p][1], 512)
        source = gw_ref.at[pl.ds(theirs, 512)]
        pending[p] = [
            send(source, pair_ref.at[p], pair_send.at[p], pair_recv.at[p], place.other_core())
        ]

    def arrive(p):
        for copy in pending[p]:
            copy.wait_recv()
        pending[p] = []

    def ring(p):
        arrive(p)
        total = gw_ref[pl.ds(first_rows[p], 512), :].astype(F32) + pair_ref[p].astype(F32)
        totals[p][0:32] = total.reshape(32, 16, D)
        axis = AXES[p][0]
        me = place.index(axis)
        for step in (1, 2, 3):
            block = lax.rem(me + step, 4) * 8
            outgoing = v_ref.at[pl.ds(1024 * p + 128 * (step - 1), 128)]
            outgoing[...] = totals[p][pl.ds(block, 8)].reshape(128, D).astype(BF16)
            slot = p * 3 + step - 1
            pending[p].append(
                send(
                    outgoing,
                    recv0.at[p, step - 1],
                    ring_send.at[slot],
                    ring_recv.at[slot],
                    place.along(**{axis: step}),
                )
            )

    def plane(p):
        arrive(p)
        axis = AXES[p][0]
        here = pl.ds(place.index(axis) * 8, 8)
        total = totals[p][here].reshape(128, D)
        for step in range(3):
            total = total + recv0[p, step].astype(F32)
        totals[p][here] = total.reshape(8, 16, D)
        first = 1024 * p + 384
        v_ref[pl.ds(first, 128), :] = total.astype(BF16)
        one, two = AXES[p][1]
        a, b = place.index(one), place.index(two)
        for k, (i, j) in enumerate(STEPS):
            block = lax.rem(a + i, 4) * 4 + lax.rem(b + j, 4)
            row = pl.multiple_of(first + block // 2 * 16, 16)
            lane = pl.multiple_of(block % 2 * 256, 256)
            slot = p * 15 + k
            pending[p].append(
                send(
                    v_ref.at[pl.ds(row, 16), pl.ds(lane, 256)],
                    recv1.at[p, k],
                    plane_send.at[slot],
                    plane_recv.at[slot],
                    place.along(**{one: i, two: j}),
                )
            )

    def plane_back(p):
        arrive(p)
        lanes = pl.ds(slot_lanes[p], 256)
        group = place.index(AXES[p][0]) * 8 + slot_rows[p] // 16
        total = totals[p][group, :, lanes]
        for k in range(15):
            total = total + recv1[p, k].astype(F32)
        row = pl.multiple_of(first_rows[p] + quarter[p] + slot_rows[p], 16)
        sum_ref[pl.ds(row, 16), lanes] = total.astype(BF16)
        here = sum_ref.at[pl.ds(row, 16), lanes]
        one, two = AXES[p][1]
        for k, (i, j) in enumerate(STEPS):
            slot = p * 15 + k
            pending[p].append(
                send(
                    here,
                    here,
                    back_send.at[slot],
                    back_recv.at[slot],
                    place.along(**{one: i, two: j}),
                )
            )

    def ring_back(p):
        arrive(p)
        here = sum_ref.at[pl.ds(pl.multiple_of(first_rows[p] + quarter[p], 128), 128)]
        for step in (1, 2, 3):
            slot = p * 3 + step - 1
            pending[p].append(
                send(
                    here,
                    here,
                    ring_back_send.at[slot],
                    ring_back_recv.at[slot],
                    place.along(**{AXES[p][0]: step}),
                )
            )

    def pair_back(p):
        arrive(p)
        here = sum_ref.at[pl.ds(first_rows[p], 512)]
        pending[p] = [send(here, here, last_send.at[p], last_recv.at[p], place.other_core())]

    gw_ref[pl.ds(0, D), :] = tn(tok_ref[own_rows, :], gq_low).astype(BF16)
    att_low = att_ref[...].reshape(768, D).astype(BF16)
    gw_ref[pl.ds(3 * D, D), :] = tn(att_low, grad_ref[...]).astype(BF16)
    exchange(0)
    gw_ref[pl.ds(D, D), :] = tn(tok_ref[...], gk_ref[...].astype(BF16)).astype(BF16)
    gw_ref[pl.ds(2 * D, D), :] = tn(tok_ref[...], gv_ref[...].astype(BF16)).astype(BF16)
    exchange(1)
    ring(0)
    u_ref[0:18] = to_tokens(pl.ds(0, 288)).reshape(18, 16, D)
    u_ref[18:36] = to_tokens(pl.ds(1056, 288)).reshape(18, 16, D)
    own = to_tokens(own_rows) + nt(gq_low, wq_ref[...])
    q_ref[...] = own.reshape(48, 16, D)
    ring(1)
    plane(0)

    for copy in along_lon:
        copy.wait_recv()

    def add_sides(ref, group, row, groups):
        for half in range(2):
            part = sides_ref[pl.ds(SIDE * half + row, 8 * groups), :].astype(F32)
            view = (pl.ds(group, groups), slice(8 * half, 8 * half + 8), slice(None))
            ref[view] = ref[view] + part.reshape(groups, 8, D)

    add_sides(u_ref, 0, 0, 18)
    add_sides(u_ref, 18, 528, 18)
    along_lat = []
    for i, dlat in enumerate((-1, 1)):
        strip = u_ref[pl.ds(18 * i, 18)].reshape(288, D).astype(BF16)
        k_ref[pl.ds(288 * i, 288), :] = strip
        copy = pltpu.make_async_remote_copy(
            src_ref=k_ref.at[pl.ds(288 * i, 288)],
            dst_ref=middle_ref.at[pl.ds(288 * i, 288)],
            send_sem=halo_send.at[2 + i],
            recv_sem=halo_recv.at[2 + i],
            device_id=place.near(dlat, 0),
            device_id_type=MESH,
        )
        guarded(place.inside[dlat], copy.start)
        along_lat.append((place.inside[dlat], place.inside[-dlat], copy))
    add_sides(q_ref, 0, 144, 48)

    plane_back(0)
    plane(1)
    ring_back(0)
    plane_back(1)
    pair_back(0)
    ring_back(1)
    pair_back(1)

    for sends, receives, copy in along_lat:
        guarded(sends, copy.wait_send)
        guarded(receives, copy.wait_recv)

    def edge(slot, first):
        rows = pl.ds(3 * first, 18)
        part = middle_ref[pl.ds(slot, 288), :].astype(F32).reshape(18, 16, D)
        q_ref[rows] = q_ref[rows] + part

    pl.when(place.lat < 7)(lambda: edge(0, 10))
    pl.when(place.lat > 0)(lambda: edge(288, 0))
    out_ref[...] = q_ref[...].reshape(768, D).astype(BF16)

    for p in range(PARTS):
        pending[p][0].wait_recv()
    for copy in waits:
        copy.wait_send()


def whole(x, g, w_query, w_key, w_value, w_out):
    dma = pltpu.SemaphoreType.DMA
    shapes = [
        ((ALL, D), BF16),
        ((768, D), BF16),
        ((4, D, D), BF16),
        ((ALL, D), BF16),
        ((ALL, D), BF16),
        ((D, 1536), BF16),
        ((D, 1536), BF16),
        ((48, 16, D), F32),
        ((48, 16, D), F32),
        ((ALL, D), F32),
        ((ALL, D), F32),
        ((48, 16, D), F32),
        ((48, 16, D), F32),
        ((6, 256, 256), BF16),
        ((6, 256, 256), BF16),
        ((6, 256, 256), BF16),
        ((2, KEYS, 384), F32),
        ((4, KEYS, 256), F32),
        ((2, KEYS, 256), BF16),
        ((KEYS, 256), BF16),
        ((4 * D, D), BF16),
        ((576, D), BF16),
        ((2 * SIDE, D), BF16),
        ((2, D, D), BF16),
    ]
    shapes += [((PARTS, 3, 128, D), BF16), ((PARTS, 15, 16, 256), BF16)]
    scratch = [pltpu.VMEM(shape, kind) for shape, kind in shapes]
    scratch.append(dma((6,)))
    for count in (8, 4, PARTS, 3 * PARTS, 15 * PARTS, 15 * PARTS, 3 * PARTS, PARTS):
        scratch += [dma((count,))] * 2
    return pl.pallas_call(
        kernel,
        out_shape=(
            jax.ShapeDtypeStruct((768, D), BF16),
            jax.ShapeDtypeStruct((4 * D, D), BF16),
        ),
        in_specs=[pl.BlockSpec(memory_space=pl.ANY)] * 6,
        out_specs=(pl.BlockSpec(memory_space=pltpu.VMEM),) * 2,
        scratch_shapes=scratch,
        compiler_params=pltpu.CompilerParams(
            collective_id=0, has_side_effects=True, vmem_limit_bytes=62 * 1024 * 1024
        ),
    )(x, g, w_query, w_key, w_value, w_out)


def on_device(tokens, w_query, w_key, w_value, w_out, grad_out):
    x = tokens.transpose(0, 2, 1, 3).reshape(768, D)
    g = grad_out.transpose(0, 2, 1, 3).reshape(768, D)
    grad_tokens, sums = whole(x, g, w_query, w_key, w_value, w_out)
    grad_tokens = grad_tokens.reshape(16, 3, 16, D).transpose(0, 2, 1, 3)
    sums = sums.reshape(4, D, D).astype(F32)
    return grad_tokens, sums[0], sums[1], sums[2], sums[3]


def solution(mesh):
    placed = (P("lat", "lon", None, None), P(), P(), P(), P(), P("lat", "lon", None, None))
    return jax.shard_map(
        on_device,
        mesh=mesh,
        in_specs=placed,
        out_specs=(P("lat", "lon", None, None), P(), P(), P(), P()),
        check_vma=False,
    )
```
